32 devices in a mesh: parts: 2 (over y), gx: 4 (over z), gy: 2 (over x), gz: 2 (over core).
Axes of the slice: x: 2, y: 2, z: 4, core: 2. Of those that a mesh axis runs over, the one named last changes fastest.
Arguments:
- positions: float32 [8, 2, 2, 3, 256], P(('parts', 'gx'), 'gy', 'gz'), parts along dimension 0, may hold values from 0 to 94
- species: int32 [8, 2, 2, 256], P(('parts', 'gx'), 'gy', 'gz'), parts along dimension 0, may hold values from 0 to 4
- neighbors: int32 [8, 2, 2, 32, 256], P(('parts', 'gx'), 'gy', 'gz'), parts along dimension 0, may hold values from -1 to 6911, as said below
- migration: int32 [8, 2, 2, 32], P(('parts', 'gx'), 'gy', 'gz'), parts along dimension 0, may hold values from -1 to 63, as said below
- latents: bfloat16 [8, 2, 2, 32, 256, 256], P(('parts', 'gx'), 'gy', 'gz'), parts along dimension 0, may hold values from -6 to 6
- w_latent: bfloat16 [256, 384], replicated, may hold values from -0.375 to 0.375
- w_tensor: bfloat16 [192, 256], replicated, may hold values from -0.4375 to 0.4375
- w_radial: float32 [8, 256], replicated, may hold values from -4 to 4
- species_center: float32 [5, 256], replicated, may hold values from -5 to 5
- species_neighbor: float32 [5, 256], replicated, may hold values from -5 to 5
- w_hidden: bfloat16 [256, 256], replicated, may hold values from -0.375 to 0.375
- w_update: bfloat16 [256, 256], replicated, may hold values from -0.375 to 0.375
- w_out: bfloat16 [256], replicated, may hold values from -0.375 to 0.375
Outputs:
- forces: float32 [8, 2, 2, 3, 128], P(('parts', 'gx'), 'gy', 'gz'), parts along dimension 0
- atom_energy: bfloat16 [8, 2, 2, 256], P(('parts', 'gx'), 'gy', 'gz'), parts along dimension 0
- latent_grad: bfloat16 [8, 2, 2, 32, 256, 256], P(('parts', 'gx'), 'gy', 'gz'), parts along dimension 0
The draws below stay inside these ranges and needn't reach their ends.
There are 2 independent parts, one for each index of `parts`. The reference program is written for one: setup_inputs(seed, part) draws one part's arguments, and reference() takes and returns one part's arrays. A program takes and returns all parts, laid end to end along the dimension named above; an argument that names none is the same for every part. Nothing has to cross between parts.
Inputs may be any that keep to these rules, and one draw needn't show every extreme that they name: `neighbors`: A home block is live where its migration entry is not -1. Entries of live centers name atoms of live blocks of devices inside the grid, never the center itself; centers in blocks that are not live have only -1. `migration`: -1 marks a block that is not live; w * 16 + s sends the block to slot s of the device with gx index w and the same gy and gz indices. Every slot of every device receives exactly one block. A device sends at most 8 blocks to one gx index; in every draw some device has all 32 blocks live and sends exactly 8 to every gx index.
All inputs are finite; a program needn't handle non-finite values.
Results may differ from the reference program's by a relative error of at most 0.01.
Values may be sent and summed in bfloat16 or wider, within the bound.
A program may use at most 128 MiB of HBM per device.

```python
import jax
import jax.numpy as jnp
import numpy as np
from jax import lax

LAT = 256
TC = 64
NB = 8
NS = 5
CB = 8
K = 32
HS = 32
WS = 16
HA = 256
EB = 256
WA = 128
N_GX = 4
N_GY = 2
N_GZ = 2


def offset_table():
    listed = []
    for step_x in range(-2, 3):
        for step_y in range(-2, 3):
            for step_z in range(-2, 3):
                square = step_x * step_x + step_y * step_y + step_z * step_z
                if 0 < square <= 4:
                    listed.append((step_x, step_y, step_z))
    return np.array(listed, dtype=np.int32)


def lattice_sites():
    atom_ids = jnp.arange(HS * CB, dtype=jnp.int32)
    block_ids = atom_ids // CB
    inner_ids = atom_ids % CB
    local_x = 2 * (block_ids % 2) + inner_ids % 2
    local_y = 2 * (block_ids // 2 % 2) + inner_ids // 2 % 2
    local_z = 2 * (block_ids // 4) + inner_ids // 4
    full_shape = (N_GX, N_GY, N_GZ, HS * CB)
    grid_x = jnp.broadcast_to(jnp.arange(N_GX, dtype=jnp.int32).reshape(-1, 1, 1, 1) * 4 + local_x, full_shape)
    grid_y = jnp.broadcast_to(jnp.arange(N_GY, dtype=jnp.int32).reshape(1, -1, 1, 1) * 4 + local_y, full_shape)
    grid_z = jnp.broadcast_to(jnp.arange(N_GZ, dtype=jnp.int32).reshape(1, 1, -1, 1) * (HS // 2) + local_z, full_shape)
    return (grid_x, grid_y, grid_z)


def live_blocks(key):
    key = jax.random.fold_in(key, 71)
    group_count = N_GY * N_GZ
    slot_total = N_GX * HS
    first_key, second_key = jax.random.split(key)
    forced = jax.random.randint(first_key, (group_count,), 0, N_GX)
    scores = jax.random.randint(second_key, (group_count, slot_total), 0, 1 << 14) * slot_total
    scores = scores + jnp.arange(slot_total, dtype=jnp.int32)[None, :]
    owners = jnp.arange(slot_total, dtype=jnp.int32) // HS
    scores = jnp.where(owners[None, :] == forced[:, None], scores - (1 << 28), scores)
    rank_of = jnp.argsort(jnp.argsort(scores, axis=1), axis=1)
    live_mask = rank_of < HS // 2 * N_GX
    return live_mask.reshape(N_GY, N_GZ, N_GX, HS).transpose(2, 0, 1, 3)


def draw_migration(key, part):
    live_mask = live_blocks(key)
    flat_live = live_mask.transpose(1, 2, 0, 3).reshape(N_GY * N_GZ, N_GX * HS).astype(jnp.int32)
    running = jnp.cumsum(flat_live, axis=1) - 1
    destination = running % N_GX * (HS // 2) + running // N_GX
    destination = jnp.where(flat_live > 0, destination, -1)
    return destination.reshape(N_GY, N_GZ, N_GX, HS).transpose(2, 0, 1, 3).astype(jnp.int32)


def draw_neighbors(key, part):
    live_mask = live_blocks(key)
    key = jax.random.fold_in(key, 9)
    grid_x, grid_y, grid_z = lattice_sites()
    offsets = jnp.asarray(offset_table())
    near_x = grid_x[..., None] + offsets[:, 0]
    near_y = grid_y[..., None] + offsets[:, 1]
    near_z = grid_z[..., None] + offsets[:, 2]
    depth = HS // 2
    inside = (near_x >= 0) & (near_x < 4 * N_GX) & (near_y >= 0) & (near_y < 4 * N_GY)
    inside = inside & (near_z >= 0) & (near_z < N_GZ * depth)
    clip_x = jnp.clip(near_x, 0, 4 * N_GX - 1)
    clip_y = jnp.clip(near_y, 0, 4 * N_GY - 1)
    clip_z = jnp.clip(near_z, 0, N_GZ * depth - 1)
    owner_x = clip_x // 4
    owner_y = clip_y // 4
    owner_z = clip_z // depth
    site_x = clip_x % 4
    site_y = clip_y % 4
    site_z = clip_z % depth
    near_block = site_x // 2 + 2 * (site_y // 2) + 4 * (site_z // 2)
    near_atom = near_block * CB + site_x % 2 + 2 * (site_y % 2) + 4 * (site_z % 2)
    near_live = live_mask[owner_x, owner_y, owner_z, near_block]
    center_live = live_mask[:, :, :, jnp.arange(HS * CB, dtype=jnp.int32) // CB]
    device_x = jnp.arange(N_GX, dtype=jnp.int32).reshape(-1, 1, 1, 1, 1)
    device_y = jnp.arange(N_GY, dtype=jnp.int32).reshape(1, -1, 1, 1, 1)
    device_z = jnp.arange(N_GZ, dtype=jnp.int32).reshape(1, 1, -1, 1, 1)
    region = (owner_x - device_x + 1) * 9 + (owner_y - device_y + 1) * 3 + (owner_z - device_z + 1)
    listed = jnp.where(inside & near_live & center_live[..., None], region * (HS * CB) + near_atom, -1)
    scores = jax.random.randint(key, listed.shape, 0, 1 << 16) * 32 + jnp.arange(32, dtype=jnp.int32)
    shuffled = jnp.take_along_axis(listed, jnp.argsort(scores, axis=-1), axis=-1)[..., :K]
    return shuffled.reshape(N_GX, N_GY, N_GZ, HS, CB * K).astype(jnp.int32)


def draw_positions(key, part):
    key = jax.random.fold_in(key, 13)
    grid_x, grid_y, grid_z = lattice_sites()
    base = jnp.stack([grid_x, grid_y, grid_z], axis=3).astype(jnp.float32) * 3.0 + 0.5
    jitter = jax.random.uniform(key, base.shape, jnp.float32, minval=-0.5, maxval=0.5)
    return base + jitter


def with_ends(values, own_key, least, largest):
    longest = values.shape.index(max(values.shape))
    spots = []
    for shift in (0, 1):
        where = [jax.random.randint(jax.random.fold_in(own_key, axis), (), 0, length) for axis, length in enumerate(values.shape)]
        where[longest] = (where[longest] + shift) % values.shape[longest]
        spots.append(tuple(where))
    return values.at[spots[0]].set(least).at[spots[1]].set(largest)


def steps_of(own_key, dims, cuts, least, top_value):
    gain = 1.0
    for dim, shards_of in cuts:
        draws = jax.random.uniform(jax.random.fold_in(jax.random.fold_in(own_key, 6), dim), (shards_of,), jnp.float32, least / len(cuts), top_value / len(cuts))
        gain = gain * jnp.repeat(jnp.exp(draws), dims[dim] // shards_of).reshape((-1,) + (1,) * (len(dims) - 1 - dim))
    return gain


def gaussian(own_key, extent, width, reach, cuts=(), kind=jnp.bfloat16):
    values = jax.random.normal(own_key, extent, jnp.float32) * width
    if len(cuts) > 0:
        values = steps_of(own_key, extent, cuts, -0.22, 0.18) * values
    return jnp.clip(values, min=-reach, max=reach).astype(kind)


def setup_inputs(seed: int = 0, part: int = 0) -> dict:
    streams_of = jax.random.split(jax.random.key(seed), 14)
    part_splits = jax.random.split(jax.random.fold_in(streams_of[13], part), 14)
    return {
        "positions": draw_positions(jax.random.fold_in(jax.random.fold_in(streams_of[13], part), 71), part),
        "species": with_ends(jax.random.randint(part_splits[1], (N_GX, N_GY, N_GZ, HA), 0, NS), jax.random.fold_in(part_splits[1], 1), 0, NS - 1).astype(jnp.int32),
        "neighbors": draw_neighbors(jax.random.fold_in(jax.random.fold_in(streams_of[13], part), 71), part),
        "migration": draw_migration(jax.random.fold_in(jax.random.fold_in(streams_of[13], part), 71), part),
        "latents": gaussian(part_splits[4], (N_GX, N_GY, N_GZ, HS, EB, LAT), 1.0, 6.0, ((0, 4), (1, 2), (2, 2))),
        "w_latent": gaussian(streams_of[5], (LAT, 2 * TC + LAT), LAT ** -0.5, 0.375),
        "w_tensor": gaussian(streams_of[6], (3 * TC, LAT), (3 * TC) ** -0.5, 0.4375),
        "w_radial": gaussian(streams_of[7], (NB, LAT), 2 ** -0.5, 4.0, (), jnp.float32),
        "species_center": gaussian(streams_of[8], (NS, LAT), 1.0, 5.0, (), jnp.float32),
        "species_neighbor": gaussian(streams_of[9], (NS, LAT), 1.0, 5.0, (), jnp.float32),
        "w_hidden": gaussian(streams_of[10], (LAT, LAT), LAT ** -0.5, 0.375),
        "w_update": gaussian(streams_of[11], (LAT, LAT), LAT ** -0.5, 0.375),
        "w_out": gaussian(streams_of[12], (LAT,), LAT ** -0.5, 0.375),
    }


cutoff_radius = 6.0
sqrt_three = 3.0 ** 0.5
sqrt_five = 5.0 ** 0.5
sqrt_fifteen = 15.0 ** 0.5

def edge_features(vectors):
    square = lax.optimization_barrier(jnp.sum(vectors * vectors, axis=0))
    length = jnp.sqrt(square)
    unit_x = vectors[0] / length
    unit_y = vectors[1] / length
    unit_z = vectors[2] / length
    envelope = jnp.maximum(1.0 - square / (cutoff_radius * cutoff_radius), 0.0) ** 2
    harmonics = jnp.stack([jnp.ones_like(length), sqrt_three * unit_x, sqrt_three * unit_y, sqrt_three * unit_z, sqrt_fifteen * unit_x * unit_y, sqrt_fifteen * unit_y * unit_z, 0.5 * sqrt_five * (3.0 * unit_z * unit_z - 1.0), sqrt_fifteen * unit_x * unit_z, 0.5 * sqrt_fifteen * (unit_x * unit_x - unit_y * unit_y)])
    orders = jnp.arange(1, NB + 1, dtype=jnp.int32).astype(vectors.dtype)
    radial = (2.0 / cutoff_radius) ** 0.5 * jnp.sin(orders[:, None] * jnp.pi * length[None, :] / cutoff_radius)
    radial = radial / length[None, :] * envelope[None, :]
    return jnp.concatenate([harmonics, radial, envelope[None, :]], axis=0)

def latent_energy(features, latent_wide, species_codes, weights):
    w_latent, w_tensor, w_radial, species_center, species_neighbor, w_hidden, w_update, w_out = weights
    channels = w_tensor.shape[0] // 3
    basis_count = w_radial.shape[0]
    species_count = species_center.shape[0]
    edge_count = latent_wide.shape[0]
    atom_count = edge_count // K
    harmonics = features[:9].T
    radial = features[9:9 + basis_count].T
    envelope = features[9 + basis_count]
    latent_low = latent_wide.astype(jnp.bfloat16)
    projected = jnp.dot(latent_low, w_latent, preferred_element_type=jnp.float32)
    env_weight = projected[:, :channels] * envelope[:, None]
    value_weight = projected[:, channels:2 * channels]
    latent_part = projected[:, 2 * channels:]
    harm_atoms = harmonics.reshape(atom_count, K, 9)
    environment = jnp.einsum('akc,akm->acm', env_weight.reshape(atom_count, K, channels), harm_atoms, precision=lax.Precision.HIGHEST) / K ** 0.5
    pieces = []
    for first_m, last_m in ((0, 1), (1, 4), (4, 9)):
        env_along = jnp.einsum('akm,acm->akc', harm_atoms[:, :, first_m:last_m], environment[:, :, first_m:last_m], precision=lax.Precision.HIGHEST)
        pieces.append(value_weight * env_along.reshape(edge_count, channels))
    invariants = jnp.concatenate(pieces, axis=1).astype(jnp.bfloat16)
    kinds = jnp.arange(species_count, dtype=jnp.int32).astype(species_codes.dtype)
    center_hot = (species_codes[0][:, None] == kinds[None, :]).astype(jnp.float32)
    neighbour_hot = (species_codes[1][:, None] == kinds[None, :]).astype(jnp.float32)
    preact = latent_part + jnp.dot(invariants, w_tensor, preferred_element_type=jnp.float32)
    preact = preact + jnp.dot(radial, w_radial, precision=lax.Precision.HIGHEST)
    preact = preact + jnp.dot(center_hot, species_center, precision=lax.Precision.HIGHEST)
    preact = preact + jnp.dot(neighbour_hot, species_neighbor, precision=lax.Precision.HIGHEST)
    hidden_one = jax.nn.silu(preact).astype(jnp.bfloat16)
    hidden_two = jax.nn.silu(jnp.dot(hidden_one, w_hidden, preferred_element_type=jnp.float32)).astype(jnp.bfloat16)
    updated = latent_wide + jnp.dot(hidden_two, w_update, preferred_element_type=jnp.float32) * envelope[:, None]
    energy = jnp.dot(updated.astype(jnp.bfloat16), w_out, preferred_element_type=jnp.float32) * envelope
    return lax.optimization_barrier(jnp.sum(energy.reshape(atom_count, K), axis=1))

def run_blocks(feature_low, species_codes, latent_block, weights):
    features = lax.optimization_barrier(feature_low).astype(jnp.float32)
    block_count = latent_block.shape[0]
    latent_wide = latent_block.reshape(block_count * latent_block.shape[1], latent_block.shape[2]).astype(jnp.float32)
    atom_energy, backward = jax.vjp(lambda feat_in, latent_in: latent_energy(feat_in, latent_in, species_codes, weights), features, latent_wide)
    feature_grad, latent_grad = backward(jnp.ones_like(atom_energy))
    return (atom_energy.astype(jnp.bfloat16), feature_grad.astype(jnp.bfloat16), latent_grad.reshape(latent_block.shape).astype(jnp.bfloat16))

def force_pull(feature_back, feature_grad_low, is_valid):
    grad_wide = lax.optimization_barrier(feature_grad_low).astype(jnp.float32)
    return feature_back(grad_wide)[0] * is_valid[None, :]

def reference(positions, species, neighbors, migration, latents, w_latent, w_tensor, w_radial, species_center, species_neighbor, w_hidden, w_update, w_out):
    weights = (w_latent, w_tensor, w_radial, species_center, species_neighbor, w_hidden, w_update, w_out)
    devices = N_GX * N_GY * N_GZ
    device_ids = jnp.arange(devices, dtype=jnp.int32)
    coord_x = device_ids // (N_GY * N_GZ)
    coord_y = device_ids // N_GZ % N_GY
    coord_z = device_ids % N_GZ
    place_all = positions.reshape(devices, 3, HA).transpose(1, 0, 2).reshape(3, devices * HA)
    kinds_all = species.reshape(devices * HA).astype(jnp.float32)
    entries = neighbors.reshape(devices, HA * K)
    is_valid = entries >= 0
    safe_entry = jnp.where(is_valid, entries, 0)
    region = safe_entry // HA
    local_atom = safe_entry % HA
    other_dev = ((coord_x[:, None] + region // 9 - 1) * N_GY + coord_y[:, None] + region // 3 % 3 - 1) * N_GZ
    other_dev = other_dev + coord_z[:, None] + region % 3 - 1
    other_id = jnp.where(is_valid, other_dev * HA + local_atom, 0).astype(jnp.int32)
    center_id = (device_ids[:, None] * HA + jnp.arange(HA * K, dtype=jnp.int32)[None, :] // K).astype(jnp.int32)
    safe_vec = jnp.array([2.0 * cutoff_radius, 0.0, 0.0], dtype=jnp.float32)
    vectors = jnp.where(is_valid[None], place_all[:, other_id] - place_all[:, center_id], safe_vec[:, None, None])
    species_codes = jnp.stack([kinds_all[center_id], jnp.where(is_valid, kinds_all[other_id], 0.0)])
    valid_wide = is_valid.astype(jnp.float32)

    def per_device(device_items):
        vec_dev, code_dev, latent_dev, valid_dev = device_items
        features, feature_back = jax.vjp(edge_features, vec_dev)
        energy_low, grad_low, latent_grad = run_blocks(features.astype(jnp.bfloat16), code_dev, latent_dev, weights)
        return (force_pull(feature_back, grad_low, valid_dev), energy_low, latent_grad)
    edge_grad, energies, latent_grads = lax.map(per_device, (vectors.transpose(1, 0, 2), species_codes.transpose(1, 0, 2), latents.reshape(devices, HS, EB, LAT), valid_wide))
    flat_grad = edge_grad.transpose(1, 0, 2).reshape(3, devices * HA * K)
    center_part = flat_grad.reshape(3, devices * HA, K).sum(axis=2)
    neighbour_part = jax.ops.segment_sum(flat_grad.T, other_id.reshape(-1), num_segments=devices * HA).T
    home_force = center_part - neighbour_part
    blocks = home_force.reshape(3, devices, HS, CB).transpose(1, 2, 0, 3).reshape(devices * HS, 3, CB)
    destinations = migration.reshape(devices, HS)
    target_dev = (destinations // WS * N_GY + coord_y[:, None]) * N_GZ + coord_z[:, None]
    target = jnp.where(destinations >= 0, target_dev * WS + destinations % WS, devices * WS).reshape(-1)
    target = target.astype(jnp.int32)
    placed = jnp.zeros((devices * WS + 1, 3, CB), jnp.float32).at[target].set(blocks)[:devices * WS]
    forces = placed.reshape(N_GX, N_GY, N_GZ, WS, 3, CB).transpose(0, 1, 2, 4, 3, 5).reshape(N_GX, N_GY, N_GZ, 3, WA)
    return (forces, energies.reshape(N_GX, N_GY, N_GZ, HA), latent_grads.reshape(N_GX, N_GY, N_GZ, HS, EB, LAT))
```

```python
import functools

import jax
import jax.numpy as jnp
import numpy as np
from jax import lax
from jax.experimental import pallas as pl
from jax.experimental.pallas import tpu as pltpu
from jax.sharding import PartitionSpec as P

NB = 8
CB = 8
K = 32
FR = 32
TILE_BLOCKS = 2

cutoff_radius = 6.0
sqrt_three = 3.0**0.5
sqrt_five = 5.0**0.5
sqrt_fifteen = 15.0**0.5
radial_scale = (2.0 / cutoff_radius) ** 0.5
f32 = jnp.float32
bf16 = jnp.bfloat16

COLUMNS = ((0, 1), (-1, 2), (-1, 3), (4, 5), (6, 7), (8, -1))


def with_halo(cells, sides, width):
    for axis, dim in sides:
        count = lax.axis_size(axis)
        ends = count - 1
        head = lax.slice_in_dim(cells, 0, width, axis=dim)
        tail = lax.slice_in_dim(cells, cells.shape[dim] - width, cells.shape[dim], axis=dim)
        cells = jnp.concatenate(
            [
                lax.ppermute(tail, axis, [(i, (i + 1) % count) for i in range(ends)]),
                cells,
                lax.ppermute(head, axis, [((i + 1) % count, i) for i in range(ends)]),
            ],
            axis=dim,
        )
    return cells


def sin_cos(angle):
    phi = angle - np.float32(np.pi / 2)
    sq = phi * phi
    cos_phi = 1.0
    coeffs = [1.0]
    for n in range(1, 8):
        coeffs.append(-coeffs[-1] / ((2 * n - 1) * (2 * n)))
    cos_phi = jnp.full_like(sq, coeffs[-1])
    for c in coeffs[-2::-1]:
        cos_phi = cos_phi * sq + c
    coeffs = [1.0]
    for n in range(1, 8):
        coeffs.append(-coeffs[-1] / ((2 * n) * (2 * n + 1)))
    sin_phi = jnp.full_like(sq, coeffs[-1])
    for c in coeffs[-2::-1]:
        sin_phi = sin_phi * sq + c
    sin_phi = sin_phi * phi
    return cos_phi, -sin_phi


def sigmoid(x):
    return 0.5 * jnp.tanh(0.5 * x) + 0.5


def dot(a, b):
    return jnp.dot(a, b, preferred_element_type=f32)


def geometry(rows, nbr_ref, own_ref, tab_ref, vec_s, feat_s):
    hs, eb = nbr_ref.shape
    lane = lax.broadcasted_iota(jnp.int32, (hs, eb), 1)
    atom = lane // K
    centers = []
    for c in range(4):
        own = own_ref[c]
        acc = jnp.broadcast_to(own[:, 0:1], (hs, eb))
        for a in range(1, CB):
            acc = jnp.where(atom == a, own[:, a : a + 1], acc)
        centers.append(acc)
    nbr = nbr_ref[...]
    valid = nbr >= 0
    safe = jnp.where(valid, nbr, 0)
    row_of = safe // 128
    lane_of = safe % 128
    halves = eb // 128

    def look(q, acc):
        out = []
        for c in range(4):
            src = jnp.broadcast_to(tab_ref[c, pl.ds(q, 1), :], (hs, 128))
            for h in range(halves):
                got = jnp.take_along_axis(
                    src, lane_of[:, h * 128 : (h + 1) * 128], axis=1, mode="promise_in_bounds"
                )
                out.append(jnp.where(row_of[:, h * 128 : (h + 1) * 128] == q, got, acc[c * halves + h]))
        return tuple(out)

    found = lax.fori_loop(
        0, rows, look, tuple(jnp.zeros((hs, 128), f32) for _ in range(4 * halves))
    )
    others = [jnp.concatenate(found[c * halves : (c + 1) * halves], axis=1) for c in range(4)]
    safe_vec = (2.0 * cutoff_radius, 0.0, 0.0)
    for c in range(3):
        vec_s[c] = jnp.where(valid, others[c] - centers[c], safe_vec[c])
    kinds_nbr = jnp.where(valid, others[3], 0.0)
    x, y, z = vec_s[0], vec_s[1], vec_s[2]
    square = x * x + y * y + z * z
    length = jnp.sqrt(square)
    inv = 1.0 / length
    ux, uy, uz = x * inv, y * inv, z * inv
    near = jnp.maximum(1.0 - square / (cutoff_radius * cutoff_radius), 0.0)
    cut = near * near
    angle = jnp.minimum(length, cutoff_radius) * np.float32(np.pi / cutoff_radius)
    sin_one, cos_one = sin_cos(angle)
    feats = [
        jnp.ones_like(x),
        sqrt_three * ux,
        sqrt_three * uy,
        sqrt_three * uz,
        sqrt_fifteen * ux * uy,
        sqrt_fifteen * uy * uz,
        0.5 * sqrt_five * (3.0 * uz * uz - 1.0),
        sqrt_fifteen * ux * uz,
        0.5 * sqrt_fifteen * (ux * ux - uy * uy),
    ]
    before, now = jnp.zeros_like(x), sin_one
    scale = radial_scale * inv * cut
    for _ in range(NB):
        feats.append(now * scale)
        before, now = now, 2.0 * cos_one * now - before
    feats.append(cut)
    for f, value in enumerate(feats):
        feat_s[:, f, :] = value.astype(bf16).astype(f32)
    base = len(feats)
    for kinds in (centers[3], kinds_nbr):
        for s in range(5):
            feat_s[:, base, :] = jnp.where(kinds == float(s), 1.0, 0.0)
            base += 1
    while base < FR:
        feat_s[:, base, :] = jnp.zeros_like(x)
        base += 1


def network(tile, lat_ref, wp, sel_y, w1, wf, wh, v2, wb, wt, wl, sel_g, wo, feat_s, grad_s, out_ref):
    first = tile * TILE_BLOCKS
    eb = lat_ref.shape[1]
    te = TILE_BLOCKS * eb
    atoms = te // K
    feat = jnp.concatenate([feat_s[first + t] for t in range(TILE_BLOCKS)], axis=1)
    feat_t = jnp.concatenate([feat, feat], axis=0).T
    env = feat_t[:, 17:18]
    feat_low = feat_t.astype(bf16)
    lat = lat_ref[...].reshape(te, lat_ref.shape[2])
    proj = dot(lat, wp[...])
    harm = dot(feat_low, sel_y[...])
    pe = proj[:, :128]
    vw = proj[:, 128:256]
    read = proj[:, 256:257]
    ew = pe * env
    norm = 1.0 / K**0.5

    def over_atom(value):
        summed = jnp.sum(value.reshape(atoms, K, 128), axis=1, keepdims=True) * norm
        return jnp.broadcast_to(summed, (atoms, K, 128)).reshape(te, 128)

    ys = [harm[:, c * 128 : (c + 1) * 128] for c in range(6)]
    envs = [over_atom(ew * yc) for yc in ys]
    ea_a = ys[0] * envs[0] + ys[1] * envs[1] + ys[2] * envs[2]
    ea_b = ys[3] * envs[3] + ys[4] * envs[4] + ys[5] * envs[5]
    inv = jnp.concatenate([(vw * ea_a).astype(bf16), (vw * ea_b).astype(bf16)], axis=1)
    p1 = dot(jnp.concatenate([lat, inv], axis=1), w1[...]) + dot(feat_low, wf[...])
    s1 = sigmoid(p1)
    h1 = p1 * s1
    d1 = s1 + h1 * (1.0 - s1)
    p2 = dot(h1.astype(bf16), wh[...])
    s2 = sigmoid(p2)
    h2 = p2 * s2
    d2 = s2 + h2 * (1.0 - s2)
    up = dot(h2.astype(bf16), v2[...])
    up = up[:, 0:1] + up[:, 1:2]
    back = dot(d2.astype(bf16), wb[...])
    g1 = ((env * env) * (d1 * back)).astype(bf16)
    gx = dot(g1, wt[...])
    gx_a, gx_b = gx[:, :128], gx[:, 128:]
    gea_a, gea_b = gx_a * vw, gx_b * vw
    gv = gx_a * ea_a + gx_b * ea_b
    gew = jnp.zeros_like(gv)
    pieces = []
    for c in range(6):
        gea = gea_a if c < 3 else gea_b
        genv = over_atom(ys[c] * gea)
        gew = gew + ys[c] * genv
        pieces.append((ew * genv + gea * envs[c]).astype(bf16))
    pieces.append(g1)
    pieces.append((pe * gew).astype(bf16))
    gf = dot(jnp.concatenate(pieces, axis=1), sel_g[...])
    lane = lax.broadcasted_iota(jnp.int32, gf.shape, 1)
    gf = gf + jnp.where(lane == 17, read + 2.0 * env * up, 0.0)
    gf = jnp.where(lane == 18, env * (read + env * up), gf)
    gft = gf.T
    for t in range(TILE_BLOCKS):
        grad_s[first + t] = gft[:, t * eb : (t + 1) * eb]
    glat = dot(
        jnp.concatenate([g1, gv.astype(bf16), (gew * env).astype(bf16)], axis=1), wl[...]
    )
    glat = glat + env * wo[...]
    out_ref[...] = glat.astype(bf16).reshape(out_ref.shape)


def pull(rows, nbr_ref, vec_s, grad_s, edge_s, part_ref, center_ref, energy_ref):
    hs, eb = nbr_ref.shape
    valid = nbr_ref[...] >= 0
    x, y, z = vec_s[0], vec_s[1], vec_s[2]
    g = [grad_s[:, f, :] for f in range(19)]
    square = x * x + y * y + z * z
    length = jnp.sqrt(square)
    inv = 1.0 / length
    ux, uy, uz = x * inv, y * inv, z * inv
    near = jnp.maximum(1.0 - square / (cutoff_radius * cutoff_radius), 0.0)
    cut = near * near
    cut_d = (-4.0 / (cutoff_radius * cutoff_radius)) * length * near
    angle = jnp.minimum(length, cutoff_radius) * np.float32(np.pi / cutoff_radius)
    sin_one, cos_one = sin_cos(angle)
    sum_sin = jnp.zeros_like(x)
    sum_cos = jnp.zeros_like(x)
    s_before, s_now = jnp.zeros_like(x), sin_one
    c_before, c_now = jnp.ones_like(x), cos_one
    for n in range(1, NB + 1):
        sum_sin = sum_sin + g[8 + n] * s_now
        sum_cos = sum_cos + (n * np.pi / cutoff_radius) * (g[8 + n] * c_now)
        s_before, s_now = s_now, 2.0 * cos_one * s_now - s_before
        c_before, c_now = c_now, 2.0 * cos_one * c_now - c_before
    along = radial_scale * inv * (cut * sum_cos + (cut_d - cut * inv) * sum_sin) + g[17] * cut_d
    gx = sqrt_three * g[1] + sqrt_fifteen * (uy * g[4] + uz * g[7] + ux * g[8])
    gy = sqrt_three * g[2] + sqrt_fifteen * (ux * g[4] + uz * g[5] - uy * g[8])
    gz = sqrt_three * g[3] + sqrt_fifteen * (uy * g[5] + ux * g[7]) + 3.0 * sqrt_five * uz * g[6]
    mixed = along - (gx * ux + gy * uy + gz * uz) * inv
    pick = (
        lax.broadcasted_iota(jnp.int32, (eb, CB), 0) // K
        == lax.broadcasted_iota(jnp.int32, (eb, CB), 1)
    ).astype(f32)
    for c, (gu, u) in enumerate(((gx, ux), (gy, uy), (gz, uz))):
        value = jnp.where(valid, gu * inv + u * mixed, 0.0)
        edge_s[c] = value
        center_ref[c] = jnp.dot(value, pick, precision=lax.Precision.HIGHEST)
    energy_ref[...] = jnp.dot(g[18], pick, precision=lax.Precision.HIGHEST)

    padded = part_ref.shape[1]
    row_iota = lax.broadcasted_iota(jnp.int32, (padded, eb), 0)
    lane_iota = lax.broadcasted_iota(jnp.int32, (128, eb), 0)
    part_ref[...] = jnp.zeros_like(part_ref)

    def scatter(b, carry):
        nbr = nbr_ref[pl.ds(b, 1), :]
        safe = jnp.where(nbr >= 0, nbr, 0)
        here = row_iota == safe // 128
        hot = jnp.where(lane_iota == safe % 128, 1.0, 0.0).astype(bf16)
        terms = []
        for c in range(3):
            value = edge_s[c, pl.ds(b, 1), :]
            high = value.astype(bf16).astype(f32)
            terms.append(jnp.where(here, high, 0.0).astype(bf16))
            terms.append(jnp.where(here, value - high, 0.0).astype(bf16))
        got = lax.dot_general(
            jnp.concatenate(terms, axis=0),
            hot,
            (((1,), (1,)), ((), ())),
            preferred_element_type=f32,
        )
        for c in range(3):
            part_ref[c] += (
                got[2 * c * padded : (2 * c + 1) * padded]
                + got[(2 * c + 1) * padded : (2 * c + 2) * padded]
            )
        return carry

    lax.fori_loop(0, hs, scatter, 0)


def kernel(
    rows, nbr, own, tab, lat, wp, sel_y, w1, wf, wh, v2, wb, wt, wl, sel_g, wo,
    out, part, center, energy, vec_s, feat_s, grad_s, edge_s,
):
    step = pl.program_id(0)

    @pl.when(step == 0)
    def _():
        geometry(rows, nbr, own, tab, vec_s, feat_s)

    network(step, lat, wp, sel_y, w1, wf, wh, v2, wb, wt, wl, sel_g, wo, feat_s, grad_s, out)

    @pl.when(step == pl.num_programs(0) - 1)
    def _():
        pull(rows, nbr, vec_s, grad_s, edge_s, part, center, energy)


def prepare(w_latent, w_tensor, w_radial, species_center, species_neighbor, w_hidden, w_update, w_out):
    tc = w_tensor.shape[0] // 3
    width = w_hidden.shape[0]
    we, wv, wlp = w_latent[:, :tc], w_latent[:, tc : 2 * tc], w_latent[:, 2 * tc :]
    wo_col = jnp.pad(w_out[:, None], ((0, 0), (0, 127)))
    wp = jnp.concatenate([we, we, wv, wv, wo_col], axis=1)
    sel_y = np.zeros((2 * FR, 128 * len(COLUMNS)), np.float32)
    for c, pair in enumerate(COLUMNS):
        for half, m in enumerate(pair):
            if m >= 0:
                sel_y[m, c * 128 + half * 64 : c * 128 + half * 64 + 64] = 1.0
    w1 = jnp.concatenate([wlp, w_tensor, w_tensor[2 * tc :]], axis=0)
    plain = jnp.concatenate(
        [
            jnp.zeros((9, width), f32),
            w_radial,
            jnp.zeros((1, width), f32),
            species_center,
            species_neighbor,
            jnp.zeros((FR - 28, width), f32),
        ],
        axis=0,
    )
    high = lax.reduce_precision(plain, 8, 7)
    wf = jnp.concatenate([high, plain - high], axis=0).astype(bf16)
    v2 = jnp.sum(w_update.astype(f32) * w_out.astype(f32)[None, :], axis=1)
    v2_high = lax.reduce_precision(v2, 8, 7)
    v2_mat = jnp.pad(jnp.stack([v2_high, v2 - v2_high], axis=1), ((0, 0), (0, 126))).astype(bf16)
    wb = (v2[:, None] * w_hidden.T.astype(f32)).astype(bf16)
    wt = jnp.concatenate([w_tensor, w_tensor[2 * tc :]], axis=0).T
    wl = jnp.concatenate([wlp.T, wv.T, wv.T, we.T, we.T], axis=0)
    fixed = np.zeros((128 * len(COLUMNS), FR), np.float32)
    for m in range(9):
        fixed[:, m] = sel_y[m]
    last = np.zeros((128, FR), np.float32)
    last[:, 17] = 1.0
    sel_g = jnp.concatenate(
        [
            jnp.asarray(fixed, bf16),
            jnp.pad(w_radial.T.astype(bf16), ((0, 0), (9, FR - 17))),
            jnp.asarray(last, bf16),
        ],
        axis=0,
    )
    return (
        wp, jnp.asarray(sel_y, bf16), w1, wf, w_hidden, v2_mat, wb, wt, wl, sel_g,
        w_out.astype(f32)[None, :],
    )


def run_device(nbr, own, tab, latents, weights):
    hs, eb, lat = latents.shape
    rows = tab.shape[1]
    padded = (rows + 7) // 8 * 8
    whole = lambda a: pl.BlockSpec(a.shape, lambda i, n=len(a.shape): (0,) * n)
    ops = (nbr, own, tab)
    block = pl.BlockSpec((TILE_BLOCKS, eb, lat), lambda i: (i, 0, 0))
    outs = (
        jax.ShapeDtypeStruct((hs, eb, lat), bf16),
        jax.ShapeDtypeStruct((3, padded, 128), f32),
        jax.ShapeDtypeStruct((3, hs, CB), f32),
        jax.ShapeDtypeStruct((hs, CB), f32),
    )
    return pl.pallas_call(
        functools.partial(kernel, rows),
        out_shape=outs,
        grid=(hs // TILE_BLOCKS,),
        in_specs=[whole(a) for a in ops] + [block] + [whole(a) for a in weights],
        out_specs=[block] + [whole(a) for a in outs[1:]],
        scratch_shapes=[
            pltpu.VMEM((3, hs, eb), f32),
            pltpu.VMEM((hs, FR, eb), f32),
            pltpu.VMEM((hs, FR, eb), f32),
            pltpu.VMEM((3, hs, eb), f32),
        ],
        compiler_params=pltpu.CompilerParams(vmem_limit_bytes=48 * 1024 * 1024),
        cost_estimate=pl.CostEstimate(
            flops=hs * eb * 1200000, bytes_accessed=4 * hs * eb * lat, transcendentals=0
        ),
    )(*ops, latents, *weights)


def per_device(
    positions, species, neighbors, migration, latents,
    w_latent, w_tensor, w_radial, species_center, species_neighbor, w_hidden, w_update, w_out,
):
    atom_count = positions.shape[-1]
    slot_count = migration.shape[-1]
    work_slots = slot_count // 2
    weights = prepare(
        w_latent, w_tensor, w_radial, species_center, species_neighbor, w_hidden, w_update, w_out
    )
    own_table = jnp.concatenate(
        [positions[0, 0, 0], species[0, 0, 0][None, :].astype(f32)], axis=0
    )
    sides = (("gx", 0), ("gy", 1), ("gz", 2))
    gathered = with_halo(own_table[None, None, None], sides, 1)
    table = gathered.transpose(3, 0, 1, 2, 4).reshape(4, 27 * atom_count // 128, 128)
    latent_grad, part, center, energy = run_device(
        neighbors[0, 0, 0],
        own_table.reshape(4, slot_count, CB),
        table,
        latents[0, 0, 0],
        weights,
    )
    rows = table.shape[1]
    region = -part[:, :rows].reshape(3, 27, atom_count)
    region = region.at[:, 13].add(center.reshape(3, atom_count))
    partial_value = region.transpose(1, 0, 2).reshape(3, 3, 3, 3, atom_count)
    padded = with_halo(partial_value.astype(bf16), sides, 1).astype(f32)
    home_force = padded[0::2, 0::2, 0::2].sum(axis=(0, 1, 2))
    moved = jnp.repeat(migration[0, 0, 0].astype(f32), CB)
    every = lax.all_gather(jnp.concatenate([home_force, moved[None]], axis=0), "gx")
    wanted = jnp.arange(work_slots * CB, dtype=jnp.int32)
    target = (lax.axis_index("gx") * work_slots + wanted // CB).astype(f32)
    inner = jnp.arange(atom_count, dtype=jnp.int32) % CB
    hot = (every[:, 3, :, None] == target) & (inner[:, None] == wanted % CB)
    forces = jnp.einsum(
        "dca,das->cs", every[:, :3], hot.astype(f32), precision=lax.Precision.HIGHEST
    )
    return (
        forces[None, None, None],
        energy.reshape(1, 1, 1, atom_count).astype(bf16),
        latent_grad[None, None, None],
    )


def solution(mesh):
    return jax.shard_map(
        per_device,
        mesh=mesh,
        in_specs=(
            P(("parts", "gx"), "gy", "gz", None, None),
            P(("parts", "gx"), "gy", "gz", None),
            P(("parts", "gx"), "gy", "gz", None, None),
            P(("parts", "gx"), "gy", "gz", None),
            P(("parts", "gx"), "gy", "gz", None, None, None),
            P(),
            P(),
            P(),
            P(),
            P(),
            P(),
            P(),
            P(),
        ),
        out_specs=(
            P(("parts", "gx"), "gy", "gz", None, None),
            P(("parts", "gx"), "gy", "gz", None),
            P(("parts", "gx"), "gy", "gz", None, None, None),
        ),
        check_vma=False,
    )
```

```python
import functools

import jax
import jax.numpy as jnp
import numpy as np
from jax import lax
from jax.experimental import pallas as pl
from jax.experimental.pallas import tpu as pltpu
from jax.sharding import PartitionSpec as P

NB = 8
CB = 8
K = 32
FR = 32
TILE_BLOCKS = 2

cutoff_radius = 6.0
sqrt_three = 3.0**0.5
sqrt_five = 5.0**0.5
sqrt_fifteen = 15.0**0.5
radial_scale = (2.0 / cutoff_radius) ** 0.5
f32 = jnp.float32
bf16 = jnp.bfloat16

COLUMNS = ((0, 1), (-1, 2), (-1, 3), (4, 5), (6, 7), (8, -1))


def near_steps(sizes):
    spans = [(-1, 0, 1) if n > 1 else (0,) for n in sizes]
    steps = [(x, y, z) for x in spans[0] for y in spans[1] for z in spans[2]]
    return [d for d in steps if d != (0, 0, 0)]


def slot_sizes(sizes):
    return tuple(min(n, 3) for n in sizes)


def slot_of(sizes, here, step):
    index = 0
    for n, at, d in zip(sizes, here, step):
        place = d + 1 if n >= 3 else (at + d if n == 2 else 0)
        index = index * min(n, 3) + place
    return index


def inside(sizes, here, step):
    ok = None
    for n, at, d in zip(sizes, here, step):
        part = None
        if d == -1:
            part = at > 0
        elif d == 1:
            part = at < n - 1
        if part is not None:
            ok = part if ok is None else jnp.logical_and(ok, part)
    return ok


def moved(here, step):
    return {"gx": here[0] + step[0], "gy": here[1] + step[1], "gz": here[2] + step[2]}


def beside(sizes, here):
    spans = []
    for n, at in zip(sizes, here):
        low = jnp.where(at > 0, 1, 0) if n > 1 else 0
        high = jnp.where(at < n - 1, 1, 0) if n > 1 else 0
        spans.append(low + high + 1)
    return spans


def spread_kernel(sizes, own_ref, out_ref, send_sem, recv_sem):
    here = tuple(lax.axis_index(n) for n in ("gx", "gy", "gz"))
    steps = near_steps(sizes)
    out_ref[...] = jnp.zeros_like(out_ref)
    out_ref[slot_of(sizes, here, (0, 0, 0))] = own_ref[...]
    barrier = pltpu.get_barrier_semaphore()
    for d in steps:
        @pl.when(inside(sizes, here, d))
        def _(d=d):
            pl.semaphore_signal(
                barrier, inc=1, device_id=moved(here, d), device_id_type=pl.DeviceIdType.MESH
            )
    spans = beside(sizes, here)
    pl.semaphore_wait(barrier, spans[0] * spans[1] * spans[2] - 1)

    def copy(n, d):
        back = tuple(-v for v in d)
        there = tuple(h + v for h, v in zip(here, d))
        return pltpu.make_async_remote_copy(
            src_ref=own_ref,
            dst_ref=out_ref.at[slot_of(sizes, there, back)],
            send_sem=send_sem.at[n],
            recv_sem=recv_sem.at[n],
            device_id=moved(here, d),
            device_id_type=pl.DeviceIdType.MESH,
        )

    for n, d in enumerate(steps):
        @pl.when(inside(sizes, here, d))
        def _(n=n, d=d):
            copy(n, d).start()
    for n, d in enumerate(steps):
        @pl.when(inside(sizes, here, d))
        def _(n=n, d=d):
            copy(n, d).wait_send()
        back = tuple(-v for v in d)

        @pl.when(inside(sizes, here, back))
        def _(n=n, back=back):
            pltpu.make_async_remote_copy(
                src_ref=own_ref,
                dst_ref=out_ref.at[slot_of(sizes, here, back)],
                send_sem=send_sem.at[n],
                recv_sem=recv_sem.at[n],
                device_id=moved(here, back),
                device_id_type=pl.DeviceIdType.MESH,
            ).wait_recv()


def collect_kernel(
    sizes, part_ref, center_ref, mig_ref, out_ref, near_ref, far_ref, s1, r1, s2, r2
):
    here = tuple(lax.axis_index(n) for n in ("gx", "gy", "gz"))
    steps = near_steps(sizes)
    ring = sizes[0]
    near_ref[...] = jnp.zeros_like(near_ref)
    shifts = list(range(1, ring))

    def peer(s):
        return {"gx": lax.rem(here[0] + s, ring), "gy": here[1], "gz": here[2]}

    barrier = pltpu.get_barrier_semaphore()
    for d in steps:
        @pl.when(inside(sizes, here, d))
        def _(d=d):
            pl.semaphore_signal(
                barrier, inc=1, device_id=moved(here, d), device_id_type=pl.DeviceIdType.MESH
            )
    for gap in [g for g in range(1 - ring, ring) if abs(g) > 1]:
        @pl.when(jnp.logical_and(here[0] + gap >= 0, here[0] + gap < ring))
        def _(gap=gap):
            pl.semaphore_signal(
                barrier,
                inc=1,
                device_id=moved(here, (gap, 0, 0)),
                device_id_type=pl.DeviceIdType.MESH,
            )
    spans = beside(sizes, here)
    pl.semaphore_wait(barrier, spans[0] * spans[1] * spans[2] - 1 + ring - spans[0])

    def give(n, d):
        return pltpu.make_async_remote_copy(
            src_ref=part_ref.at[slot_of(sizes, here, d)],
            dst_ref=near_ref.at[n],
            send_sem=s1.at[n],
            recv_sem=r1.at[n],
            device_id=moved(here, d),
            device_id_type=pl.DeviceIdType.MESH,
        )

    for n, d in enumerate(steps):
        @pl.when(inside(sizes, here, d))
        def _(n=n, d=d):
            give(n, d).start()
    for n, d in enumerate(steps):
        back = tuple(-v for v in d)

        @pl.when(inside(sizes, here, back))
        def _(n=n, back=back):
            pltpu.make_async_remote_copy(
                src_ref=center_ref,
                dst_ref=near_ref.at[n],
                send_sem=s1.at[n],
                recv_sem=r1.at[n],
                device_id=moved(here, back),
                device_id_type=pl.DeviceIdType.MESH,
            ).wait_recv()
    force = center_ref[...] - part_ref[slot_of(sizes, here, (0, 0, 0))]
    for n in range(len(steps)):
        force = force - near_ref[n]
    row = lax.broadcasted_iota(jnp.int32, force.shape, 0)
    mig = mig_ref[...]
    force = jnp.where(row == 6, mig[0:1], jnp.where(row == 7, mig[1:2], force))
    far_ref[0] = force

    def pass_on(s):
        return pltpu.make_async_remote_copy(
            src_ref=far_ref.at[0],
            dst_ref=far_ref.at[s],
            send_sem=s2.at[s],
            recv_sem=r2.at[s],
            device_id=peer(s),
            device_id_type=pl.DeviceIdType.MESH,
        )

    for s in shifts:
        pass_on(s).start()
    slots = lax.broadcasted_iota(jnp.int32, (128, 128), 0)
    lanes = lax.broadcasted_iota(jnp.int32, (128, 128), 1)
    same = slots % CB == lanes % CB
    target = (here[0] * (128 // CB) + slots // CB).astype(f32)
    total = jnp.zeros((8, 128), f32)
    for s in range(ring):
        if s > 0:
            pass_on(s).wait_recv()
        block = far_ref[s]
        for h in range(2):
            hot = jnp.where((block[6 + h : 7 + h] == target) & same, 1.0, 0.0)
            mine = jnp.where(row % 2 == h, block, 0.0)
            total = total + lax.dot_general(
                mine, hot, (((1,), (1,)), ((), ())), precision=lax.Precision.HIGHEST,
                preferred_element_type=f32,
            )
    for c in range(3):
        out_ref[c : c + 1, :] = total[2 * c : 2 * c + 1] + total[2 * c + 1 : 2 * c + 2]
    for s in shifts:
        pass_on(s).wait_send()
    for n, d in enumerate(steps):
        @pl.when(inside(sizes, here, d))
        def _(n=n, d=d):
            give(n, d).wait_send()


def spread(own, sizes):
    count = len(near_steps(sizes))
    total = int(np.prod(slot_sizes(sizes)))
    return pl.pallas_call(
        functools.partial(spread_kernel, sizes),
        out_shape=jax.ShapeDtypeStruct((total, 8, 128), f32),
        in_specs=[pl.BlockSpec(memory_space=pltpu.VMEM)],
        out_specs=pl.BlockSpec(memory_space=pltpu.VMEM),
        scratch_shapes=[pltpu.SemaphoreType.DMA((count,)), pltpu.SemaphoreType.DMA((count,))],
        compiler_params=pltpu.CompilerParams(collective_id=0, has_side_effects=True),
    )(own)


def collect(part, center, mig, sizes):
    count = len(near_steps(sizes))
    dma = pltpu.SemaphoreType.DMA
    return pl.pallas_call(
        functools.partial(collect_kernel, sizes),
        out_shape=jax.ShapeDtypeStruct((3, 128), f32),
        in_specs=[pl.BlockSpec(memory_space=pltpu.VMEM)] * 3,
        out_specs=pl.BlockSpec(memory_space=pltpu.VMEM),
        scratch_shapes=[
            pltpu.VMEM((count, 8, 128), f32),
            pltpu.VMEM((sizes[0], 8, 128), f32),
            dma((count,)), dma((count,)), dma((sizes[0],)), dma((sizes[0],)),
        ],
        compiler_params=pltpu.CompilerParams(collective_id=1, has_side_effects=True),
    )(part, center, mig)


def places(sizes, nbr):
    here = tuple(lax.axis_index(n) for n in ("gx", "gy", "gz"))
    safe = jnp.where(nbr >= 0, nbr, 0)
    region = safe // 256
    step = (region // 9 - 1, region // 3 % 3 - 1, region % 3 - 1)
    slot = 0
    for n, at, d in zip(sizes, here, step):
        place = d + 1 if n >= 3 else (at + d if n == 2 else 0)
        slot = slot * min(n, 3) + place
    return slot, safe // 128 % 2, safe % 128


def sin_cos(angle):
    phi = angle - np.float32(np.pi / 2)
    sq = phi * phi
    cos_phi = 1.0
    coeffs = [1.0]
    for n in range(1, 8):
        coeffs.append(-coeffs[-1] / ((2 * n - 1) * (2 * n)))
    cos_phi = jnp.full_like(sq, coeffs[-1])
    for c in coeffs[-2::-1]:
        cos_phi = cos_phi * sq + c
    coeffs = [1.0]
    for n in range(1, 8):
        coeffs.append(-coeffs[-1] / ((2 * n) * (2 * n + 1)))
    sin_phi = jnp.full_like(sq, coeffs[-1])
    for c in coeffs[-2::-1]:
        sin_phi = sin_phi * sq + c
    sin_phi = sin_phi * phi
    return cos_phi, -sin_phi


def sigmoid(x):
    return 0.5 * jnp.tanh(0.5 * x) + 0.5


def dot(a, b):
    return jnp.dot(a, b, preferred_element_type=f32)


def geometry(sizes, nbr_ref, own_ref, tab_ref, vec_s, feat_s, code_s):
    hs, eb = nbr_ref.shape
    lane = lax.broadcasted_iota(jnp.int32, (hs, eb), 1)
    atom = lane // K
    centers = []
    for c in range(4):
        own = own_ref[c]
        acc = jnp.broadcast_to(own[:, 0:1], (hs, eb))
        for a in range(1, CB):
            acc = jnp.where(atom == a, own[:, a : a + 1], acc)
        centers.append(acc)
    nbr = nbr_ref[...]
    valid = nbr >= 0
    slot, half, lane_of = places(sizes, nbr)
    row_of = slot * 2 + half
    code_s[0] = slot
    code_s[1] = half
    code_s[2] = lane_of
    halves = eb // 128

    def look(q, acc):
        out = list(acc)
        for k in range(2):
            for c in range(4):
                src = jnp.broadcast_to(tab_ref[q, pl.ds(2 * c + k, 1), :], (hs, 128))
                for h in range(halves):
                    cols = slice(h * 128, (h + 1) * 128)
                    got = jnp.take_along_axis(
                        src, lane_of[:, cols], axis=1, mode="promise_in_bounds"
                    )
                    out[c * halves + h] = jnp.where(
                        row_of[:, cols] == 2 * q + k, got, out[c * halves + h]
                    )
        return tuple(out)

    found = lax.fori_loop(
        0, tab_ref.shape[0], look, tuple(jnp.zeros((hs, 128), f32) for _ in range(4 * halves))
    )
    others = [jnp.concatenate(found[c * halves : (c + 1) * halves], axis=1) for c in range(4)]
    safe_vec = (2.0 * cutoff_radius, 0.0, 0.0)
    for c in range(3):
        vec_s[c] = jnp.where(valid, others[c] - centers[c], safe_vec[c])
    kinds_nbr = jnp.where(valid, others[3], 0.0)
    x, y, z = vec_s[0], vec_s[1], vec_s[2]
    square = x * x + y * y + z * z
    length = jnp.sqrt(square)
    inv = 1.0 / length
    ux, uy, uz = x * inv, y * inv, z * inv
    near = jnp.maximum(1.0 - square / (cutoff_radius * cutoff_radius), 0.0)
    cut = near * near
    angle = jnp.minimum(length, cutoff_radius) * np.float32(np.pi / cutoff_radius)
    sin_one, cos_one = sin_cos(angle)
    feats = [
        jnp.ones_like(x),
        sqrt_three * ux,
        sqrt_three * uy,
        sqrt_three * uz,
        sqrt_fifteen * ux * uy,
        sqrt_fifteen * uy * uz,
        0.5 * sqrt_five * (3.0 * uz * uz - 1.0),
        sqrt_fifteen * ux * uz,
        0.5 * sqrt_fifteen * (ux * ux - uy * uy),
    ]
    before, now = jnp.zeros_like(x), sin_one
    scale = radial_scale * inv * cut
    for _ in range(NB):
        feats.append(now * scale)
        before, now = now, 2.0 * cos_one * now - before
    feats.append(cut)
    for f, value in enumerate(feats):
        feat_s[:, f, :] = value.astype(bf16).astype(f32)
    base = len(feats)
    for kinds in (centers[3], kinds_nbr):
        for s in range(5):
            feat_s[:, base, :] = jnp.where(kinds == float(s), 1.0, 0.0)
            base += 1
    while base < FR:
        feat_s[:, base, :] = jnp.zeros_like(x)
        base += 1


def network(tile, lat_ref, wp, sel_y, w1, wf, wh, v2, wb, wt, wl, sel_g, wo, feat_s, grad_s, out_ref):
    first = tile * TILE_BLOCKS
    eb = lat_ref.shape[1]
    te = TILE_BLOCKS * eb
    atoms = te // K
    feat = jnp.concatenate([feat_s[first + t] for t in range(TILE_BLOCKS)], axis=1)
    feat_t = jnp.concatenate([feat, feat], axis=0).T
    env = feat_t[:, 17:18]
    feat_low = feat_t.astype(bf16)
    lat = lat_ref[...].reshape(te, lat_ref.shape[2])
    proj = dot(lat, wp[...])
    harm = dot(feat_low, sel_y[...])
    pe = proj[:, :128]
    vw = proj[:, 128:256]
    read = proj[:, 256:257]
    ew = pe * env
    norm = 1.0 / K**0.5

    def over_atom(value):
        summed = jnp.sum(value.reshape(atoms, K, 128), axis=1, keepdims=True) * norm
        return jnp.broadcast_to(summed, (atoms, K, 128)).reshape(te, 128)

    ys = [harm[:, c * 128 : (c + 1) * 128] for c in range(6)]
    envs = [over_atom(ew * yc) for yc in ys]
    ea_a = ys[0] * envs[0] + ys[1] * envs[1] + ys[2] * envs[2]
    ea_b = ys[3] * envs[3] + ys[4] * envs[4] + ys[5] * envs[5]
    inv = jnp.concatenate([(vw * ea_a).astype(bf16), (vw * ea_b).astype(bf16)], axis=1)
    p1 = dot(jnp.concatenate([lat, inv], axis=1), w1[...]) + dot(feat_low, wf[...])
    s1 = sigmoid(p1)
    h1 = p1 * s1
    d1 = s1 + h1 * (1.0 - s1)
    p2 = dot(h1.astype(bf16), wh[...])
    s2 = sigmoid(p2)
    h2 = p2 * s2
    d2 = s2 + h2 * (1.0 - s2)
    up = dot(h2.astype(bf16), v2[...])
    up = up[:, 0:1] + up[:, 1:2]
    back = dot(d2.astype(bf16), wb[...])
    g1 = ((env * env) * (d1 * back)).astype(bf16)
    gx = dot(g1, wt[...])
    gx_a, gx_b = gx[:, :128], gx[:, 128:]
    gea_a, gea_b = gx_a * vw, gx_b * vw
    gv = gx_a * ea_a + gx_b * ea_b
    gew = jnp.zeros_like(gv)
    pieces = []
    for c in range(6):
        gea = gea_a if c < 3 else gea_b
        genv = over_atom(ys[c] * gea)
        gew = gew + ys[c] * genv
        pieces.append((ew * genv + gea * envs[c]).astype(bf16))
    pieces.append(g1)
    pieces.append((pe * gew).astype(bf16))
    gf = dot(jnp.concatenate(pieces, axis=1), sel_g[...])
    lane = lax.broadcasted_iota(jnp.int32, gf.shape, 1)
    gf = gf + jnp.where(lane == 17, read + 2.0 * env * up, 0.0)
    gf = jnp.where(lane == 18, env * (read + env * up), gf)
    gft = gf.T
    for t in range(TILE_BLOCKS):
        grad_s[first + t] = gft[:, t * eb : (t + 1) * eb]
    glat = dot(
        jnp.concatenate([g1, gv.astype(bf16), (gew * env).astype(bf16)], axis=1), wl[...]
    )
    glat = glat + env * wo[...]
    out_ref[...] = glat.astype(bf16).reshape(out_ref.shape)


def pull(nbr_ref, vec_s, grad_s, edge_s, code_s, part_ref, center_ref):
    hs, eb = nbr_ref.shape
    valid = nbr_ref[...] >= 0
    x, y, z = vec_s[0], vec_s[1], vec_s[2]
    g = [grad_s[:, f, :] for f in range(19)]
    square = x * x + y * y + z * z
    length = jnp.sqrt(square)
    inv = 1.0 / length
    ux, uy, uz = x * inv, y * inv, z * inv
    near = jnp.maximum(1.0 - square / (cutoff_radius * cutoff_radius), 0.0)
    cut = near * near
    cut_d = (-4.0 / (cutoff_radius * cutoff_radius)) * length * near
    angle = jnp.minimum(length, cutoff_radius) * np.float32(np.pi / cutoff_radius)
    sin_one, cos_one = sin_cos(angle)
    sum_sin = jnp.zeros_like(x)
    sum_cos = jnp.zeros_like(x)
    s_before, s_now = jnp.zeros_like(x), sin_one
    c_before, c_now = jnp.ones_like(x), cos_one
    for n in range(1, NB + 1):
        sum_sin = sum_sin + g[8 + n] * s_now
        sum_cos = sum_cos + (n * np.pi / cutoff_radius) * (g[8 + n] * c_now)
        s_before, s_now = s_now, 2.0 * cos_one * s_now - s_before
        c_before, c_now = c_now, 2.0 * cos_one * c_now - c_before
    along = radial_scale * inv * (cut * sum_cos + (cut_d - cut * inv) * sum_sin) + g[17] * cut_d
    gx = sqrt_three * g[1] + sqrt_fifteen * (uy * g[4] + uz * g[7] + ux * g[8])
    gy = sqrt_three * g[2] + sqrt_fifteen * (ux * g[4] + uz * g[5] - uy * g[8])
    gz = sqrt_three * g[3] + sqrt_fifteen * (uy * g[5] + ux * g[7]) + 3.0 * sqrt_five * uz * g[6]
    mixed = along - (gx * ux + gy * uy + gz * uz) * inv
    for c, (gu, u) in enumerate(((gx, ux), (gy, uy), (gz, uz))):
        value = jnp.where(valid, gu * inv + u * mixed, 0.0)
        edge_s[c] = value
    edge_s[3] = g[18]

    count = part_ref.shape[0]
    row = lax.broadcasted_iota(jnp.int32, (8, eb), 0)
    lane_iota = lax.broadcasted_iota(jnp.int32, (128, eb), 0)
    atom = lax.broadcasted_iota(jnp.int32, (128, eb), 1) // K
    per_half = hs // 2
    part_ref[...] = jnp.zeros_like(part_ref)
    center_ref[...] = jnp.zeros_like(center_ref)

    def across(values, hot):
        got = lax.dot_general(
            values.astype(bf16), hot, (((1,), (1,)), ((), ())), preferred_element_type=f32
        )
        mid = got.shape[0] // 2
        return got[:mid] + got[mid:]

    def scatter(b, carry):
        slot, half, lane = (code_s[c, pl.ds(b, 1), :] for c in range(3))
        hot = jnp.where(lane_iota == lane, 1.0, 0.0).astype(bf16)
        own_hot = jnp.where(lane_iota == b % per_half * CB + atom, 1.0, 0.0).astype(bf16)
        value = edge_s[3, pl.ds(b, 1), :]
        value = jnp.broadcast_to(value, (8, eb))
        for c in range(3):
            value = jnp.where(row // 2 == c, edge_s[c, pl.ds(b, 1), :], value)
        high = value.astype(bf16).astype(f32)
        low = value - high
        own = row % 2 == b // per_half
        center_ref[...] += across(
            jnp.concatenate([jnp.where(own, high, 0.0), jnp.where(own, low, 0.0)], axis=0),
            own_hot,
        )
        there = row % 2 == half
        high = jnp.where(there, high, 0.0)
        low = jnp.where(there, low, 0.0)
        terms = [jnp.where(slot == q, high, 0.0) for q in range(count)]
        terms += [jnp.where(slot == q, low, 0.0) for q in range(count)]
        part_ref[...] += across(jnp.concatenate(terms, axis=0), hot).reshape(part_ref.shape)
        return carry

    lax.fori_loop(0, hs, scatter, 0)


def prepare(wlat, wten, wrad, wcen, wnei, whid, wupd, wout, sel, wp, w1, wf, v2, wb, wt, wl, sel_g, plain_s):
    tc = wten.shape[0] // 3
    wide = wlat[...].astype(f32)
    first, rest = wide[:, : 2 * tc], wide[:, 2 * tc :]
    turned = jnp.concatenate([first[:, tc:], first[:, :tc]], axis=1)
    lane = lax.broadcasted_iota(jnp.int32, first.shape, 1)
    we = jnp.where(lane < tc, first, turned)
    wv = jnp.where(lane < tc, turned, first)
    out_row = wout[...].astype(f32)
    wp[:, 0:128] = we.astype(bf16)
    wp[:, 128:256] = wv.astype(bf16)
    wp[:, 256:384] = jnp.broadcast_to(out_row, (128, out_row.shape[1])).T.astype(bf16)
    n = wide.shape[0]
    w1[0:n] = wlat[:, 2 * tc :]
    w1[n : n + 3 * tc] = wten[...]
    w1[n + 3 * tc : n + 4 * tc] = wten[2 * tc :]
    wl[0:n] = rest.T.astype(bf16)
    wl[n : n + 128] = wv.T.astype(bf16)
    wl[n + 128 : n + 256] = we.T.astype(bf16)
    ten = wten[...].astype(f32)
    wt[...] = jnp.concatenate([ten, ten[2 * tc :]], axis=0).T.astype(bf16)
    plain_s[...] = jnp.zeros_like(plain_s)
    plain_s[9:17] = wrad[...]
    sel_g[0 : sel.shape[0]] = sel[...].astype(bf16)
    at = sel.shape[0]
    sel_g[at : at + n] = plain_s[...].T.astype(bf16)
    tail = lax.broadcasted_iota(jnp.int32, (128, FR), 1)
    sel_g[at + n : at + n + 128] = jnp.where(tail == 17, 1.0, 0.0).astype(bf16)
    plain_s[18:23] = wcen[...]
    plain_s[23:28] = wnei[...]
    plain = plain_s[...]
    high = plain.astype(bf16).astype(f32)
    wf[0:FR] = high.astype(bf16)
    wf[FR : 2 * FR] = (plain - high).astype(bf16)
    col = jnp.sum(wupd[...].astype(f32) * out_row, axis=1, keepdims=True)
    col_high = col.astype(bf16).astype(f32)
    lane = lax.broadcasted_iota(jnp.int32, (n, 128), 1)
    v2[...] = jnp.where(
        lane == 0, col_high, jnp.where(lane == 1, col - col_high, 0.0)
    ).astype(bf16)
    wb[...] = (col * whid[...].astype(f32).T).astype(bf16)


def kernel(
    sizes, nbr, own, tab, lat, sel_y, sel, wlat, wten, wrad, wcen, wnei, whid, wupd, wout,
    out, part, center,
    vec_s, feat_s, grad_s, edge_s, code_s, wp, w1, wf, v2, wb, wt, wl, sel_g, wo, plain_s,
):
    step = pl.program_id(0)

    @pl.when(step == 0)
    def _():
        prepare(
            wlat, wten, wrad, wcen, wnei, whid, wupd, wout, sel,
            wp, w1, wf, v2, wb, wt, wl, sel_g, plain_s,
        )
        wo[...] = wout[...].astype(f32)
        geometry(sizes, nbr, own, tab, vec_s, feat_s, code_s)

    network(step, lat, wp, sel_y, w1, wf, whid, v2, wb, wt, wl, sel_g, wo, feat_s, grad_s, out)

    @pl.when(step == pl.num_programs(0) - 1)
    def _():
        pull(nbr, vec_s, grad_s, edge_s, code_s, part, center)


def run_device(nbr, own, tab, latents, weights, sizes):
    hs, eb, lat = latents.shape
    whole = lambda a: pl.BlockSpec(a.shape, lambda i, n=len(a.shape): (0,) * n)
    ops = (nbr, own, tab)
    wide = 128 * len(COLUMNS)
    sel_y = np.zeros((2 * FR, wide), np.float32)
    for c, pair in enumerate(COLUMNS):
        for half, m in enumerate(pair):
            if m >= 0:
                sel_y[m, c * 128 + half * 64 : c * 128 + half * 64 + 64] = 1.0
    fixed = np.zeros((wide, FR), np.float32)
    fixed[:, :9] = sel_y[:9].T
    weights = (jnp.asarray(sel_y, bf16), jnp.asarray(fixed, bf16)) + weights
    block = pl.BlockSpec((TILE_BLOCKS, eb, lat), lambda i: (i, 0, 0))
    outs = (
        jax.ShapeDtypeStruct((hs, eb, lat), bf16),
        jax.ShapeDtypeStruct(tab.shape, f32),
        jax.ShapeDtypeStruct((8, 128), f32),
    )
    return pl.pallas_call(
        functools.partial(kernel, sizes),
        out_shape=outs,
        grid=(hs // TILE_BLOCKS,),
        in_specs=[whole(a) for a in ops] + [block] + [whole(a) for a in weights],
        out_specs=[block] + [whole(a) for a in outs[1:]],
        scratch_shapes=[
            pltpu.VMEM((3, hs, eb), f32),
            pltpu.VMEM((hs, FR, eb), f32),
            pltpu.VMEM((hs, FR, eb), f32),
            pltpu.VMEM((4, hs, eb), f32),
            pltpu.VMEM((3, hs, eb), jnp.int32),
            pltpu.VMEM((lat, 384), bf16),
            pltpu.VMEM((2 * lat, lat), bf16),
            pltpu.VMEM((2 * FR, lat), bf16),
            pltpu.VMEM((lat, 128), bf16),
            pltpu.VMEM((lat, lat), bf16),
            pltpu.VMEM((lat, lat), bf16),
            pltpu.VMEM((2 * lat, lat), bf16),
            pltpu.VMEM((wide + lat + 128, FR), bf16),
            pltpu.VMEM((1, lat), f32),
            pltpu.VMEM((FR, lat), f32),
        ],
        compiler_params=pltpu.CompilerParams(vmem_limit_bytes=48 * 1024 * 1024),
        cost_estimate=pl.CostEstimate(
            flops=hs * eb * 1200000, bytes_accessed=4 * hs * eb * lat, transcendentals=0
        ),
    )(*ops, latents, *weights)


def per_device(
    positions, species, neighbors, migration, latents,
    w_latent, w_tensor, w_radial, species_center, species_neighbor, w_hidden, w_update, w_out,
):
    atom_count = positions.shape[-1]
    slot_count = migration.shape[-1]
    sizes = tuple(lax.axis_size(n) for n in ("gx", "gy", "gz"))
    weights = (
        w_latent, w_tensor, w_radial, species_center, species_neighbor, w_hidden, w_update,
        w_out[None, :],
    )
    own_table = jnp.concatenate(
        [positions[0, 0, 0], species[0, 0, 0][None, :].astype(f32)], axis=0
    )
    table = spread(own_table.reshape(8, 128), sizes)
    latent_grad, part, center = run_device(
        neighbors[0, 0, 0],
        own_table.reshape(4, slot_count, CB),
        table,
        latents[0, 0, 0],
        weights,
        sizes,
    )
    mig = jnp.broadcast_to(migration[0, 0, 0].astype(f32)[:, None], (slot_count, CB))
    forces = collect(part, center, mig.reshape(2, 128), sizes)
    return (
        forces[None, None, None],
        center[6:8].reshape(1, 1, 1, atom_count).astype(bf16),
        latent_grad[None, None, None],
    )


def solution(mesh):
    return jax.shard_map(
        per_device,
        mesh=mesh,
        in_specs=(
            P(("parts", "gx"), "gy", "gz", None, None),
            P(("parts", "gx"), "gy", "gz", None),
            P(("parts", "gx"), "gy", "gz", None, None),
            P(("parts", "gx"), "gy", "gz", None),
            P(("parts", "gx"), "gy", "gz", None, None, None),
            P(),
            P(),
            P(),
            P(),
            P(),
            P(),
            P(),
            P(),
        ),
        out_specs=(
            P(("parts", "gx"), "gy", "gz", None, None),
            P(("parts", "gx"), "gy", "gz", None),
            P(("parts", "gx"), "gy", "gz", None, None, None),
        ),
        check_vma=False,
    )
```

```python
import functools

import jax
import jax.numpy as jnp
import numpy as np
from jax import lax
from jax.experimental import pallas as pl
from jax.experimental.pallas import tpu as pltpu
from jax.sharding import PartitionSpec as P

NB = 8
CB = 8
K = 32
FR = 32
TILE_BLOCKS = 4

cutoff_radius = 6.0
sqrt_three = 3.0**0.5
sqrt_five = 5.0**0.5
sqrt_fifteen = 15.0**0.5
radial_scale = (2.0 / cutoff_radius) ** 0.5
f32 = jnp.float32
bf16 = jnp.bfloat16

COLUMNS = ((0, 1), (-1, 2), (-1, 3), (4, 5), (6, 7), (8, -1))


def near_steps(sizes):
    spans = [(-1, 0, 1) if n > 1 else (0,) for n in sizes]
    steps = [(x, y, z) for x in spans[0] for y in spans[1] for z in spans[2]]
    return [d for d in steps if d != (0, 0, 0)]


def slot_sizes(sizes):
    return tuple(min(n, 3) for n in sizes)


def slot_of(sizes, here, step):
    index = 0
    for n, at, d in zip(sizes, here, step):
        place = d + 1 if n >= 3 else (at + d if n == 2 else 0)
        index = index * min(n, 3) + place
    return index


def inside(sizes, here, step):
    ok = None
    for n, at, d in zip(sizes, here, step):
        part = None
        if d == -1:
            part = at > 0
        elif d == 1:
            part = at < n - 1
        if part is not None:
            ok = part if ok is None else jnp.logical_and(ok, part)
    return ok


def moved(here, step):
    return {"gx": here[0] + step[0], "gy": here[1] + step[1], "gz": here[2] + step[2]}


def beside(sizes, here):
    spans = []
    for n, at in zip(sizes, here):
        low = jnp.where(at > 0, 1, 0) if n > 1 else 0
        high = jnp.where(at < n - 1, 1, 0) if n > 1 else 0
        spans.append(low + high + 1)
    return spans


def spread_kernel(sizes, pos_ref, kind_ref, out_ref, own_ref, send_sem, recv_sem):
    here = tuple(lax.axis_index(n) for n in ("gx", "gy", "gz"))
    steps = near_steps(sizes)
    out_ref[...] = jnp.zeros_like(out_ref)
    for c in range(4):
        line = pos_ref[c : c + 1, :] if c < 3 else kind_ref[...].astype(f32)
        for h in range(2):
            own_ref[2 * c + h : 2 * c + h + 1, :] = line[:, h * 128 : (h + 1) * 128]
    out_ref[slot_of(sizes, here, (0, 0, 0))] = own_ref[...]
    barrier = pltpu.get_barrier_semaphore()
    for d in steps:
        @pl.when(inside(sizes, here, d))
        def _(d=d):
            pl.semaphore_signal(
                barrier, inc=1, device_id=moved(here, d), device_id_type=pl.DeviceIdType.MESH
            )
    spans = beside(sizes, here)
    pl.semaphore_wait(barrier, spans[0] * spans[1] * spans[2] - 1)

    def copy(n, d):
        back = tuple(-v for v in d)
        there = tuple(h + v for h, v in zip(here, d))
        return pltpu.make_async_remote_copy(
            src_ref=own_ref,
            dst_ref=out_ref.at[slot_of(sizes, there, back)],
            send_sem=send_sem.at[n],
            recv_sem=recv_sem.at[n],
            device_id=moved(here, d),
            device_id_type=pl.DeviceIdType.MESH,
        )

    for n, d in enumerate(steps):
        @pl.when(inside(sizes, here, d))
        def _(n=n, d=d):
            copy(n, d).start()
    for n, d in enumerate(steps):
        @pl.when(inside(sizes, here, d))
        def _(n=n, d=d):
            copy(n, d).wait_send()
        back = tuple(-v for v in d)

        @pl.when(inside(sizes, here, back))
        def _(n=n, back=back):
            pltpu.make_async_remote_copy(
                src_ref=own_ref,
                dst_ref=out_ref.at[slot_of(sizes, here, back)],
                send_sem=send_sem.at[n],
                recv_sem=recv_sem.at[n],
                device_id=moved(here, back),
                device_id_type=pl.DeviceIdType.MESH,
            ).wait_recv()


def collect_kernel(
    sizes, part_ref, center_ref, mig_ref, out_ref, near_ref, far_ref, s1, r1, s2, r2
):
    here = tuple(lax.axis_index(n) for n in ("gx", "gy", "gz"))
    steps = near_steps(sizes)
    ring = sizes[0]
    near_ref[...] = jnp.zeros_like(near_ref)
    shifts = list(range(1, ring))

    def peer(s):
        return {"gx": lax.rem(here[0] + s, ring), "gy": here[1], "gz": here[2]}

    barrier = pltpu.get_barrier_semaphore()
    for d in steps:
        @pl.when(inside(sizes, here, d))
        def _(d=d):
            pl.semaphore_signal(
                barrier, inc=1, device_id=moved(here, d), device_id_type=pl.DeviceIdType.MESH
            )
    for gap in [g for g in range(1 - ring, ring) if abs(g) > 1]:
        @pl.when(jnp.logical_and(here[0] + gap >= 0, here[0] + gap < ring))
        def _(gap=gap):
            pl.semaphore_signal(
                barrier,
                inc=1,
                device_id=moved(here, (gap, 0, 0)),
                device_id_type=pl.DeviceIdType.MESH,
            )
    spans = beside(sizes, here)
    pl.semaphore_wait(barrier, spans[0] * spans[1] * spans[2] - 1 + ring - spans[0])

    def give(n, d):
        return pltpu.make_async_remote_copy(
            src_ref=part_ref.at[slot_of(sizes, here, d)],
            dst_ref=near_ref.at[n],
            send_sem=s1.at[n],
            recv_sem=r1.at[n],
            device_id=moved(here, d),
            device_id_type=pl.DeviceIdType.MESH,
        )

    for n, d in enumerate(steps):
        @pl.when(inside(sizes, here, d))
        def _(n=n, d=d):
            give(n, d).start()
    for n, d in enumerate(steps):
        back = tuple(-v for v in d)

        @pl.when(inside(sizes, here, back))
        def _(n=n, back=back):
            pltpu.make_async_remote_copy(
                src_ref=center_ref,
                dst_ref=near_ref.at[n],
                send_sem=s1.at[n],
                recv_sem=r1.at[n],
                device_id=moved(here, back),
                device_id_type=pl.DeviceIdType.MESH,
            ).wait_recv()
    force = center_ref[...] - part_ref[slot_of(sizes, here, (0, 0, 0))]
    for n in range(len(steps)):
        force = force - near_ref[n]
    row = lax.broadcasted_iota(jnp.int32, force.shape, 0)
    hs = mig_ref.shape[1]
    kept = lax.broadcasted_iota(jnp.int32, (8, hs), 1) // (hs // 2) == (
        lax.broadcasted_iota(jnp.int32, (8, hs), 0) % 2
    )
    mig = jnp.where(kept, mig_ref[...].astype(f32), 0.0)
    widen = (
        lax.broadcasted_iota(jnp.int32, (hs, 128), 1) // CB
        == lax.broadcasted_iota(jnp.int32, (hs, 128), 0) % (hs // 2)
    )
    mig = jnp.dot(
        mig, jnp.where(widen, 1.0, 0.0), precision=lax.Precision.HIGHEST,
        preferred_element_type=f32,
    )
    force = jnp.where(row >= 6, mig, force)
    far_ref[0] = force

    def pass_on(s):
        return pltpu.make_async_remote_copy(
            src_ref=far_ref.at[0],
            dst_ref=far_ref.at[s],
            send_sem=s2.at[s],
            recv_sem=r2.at[s],
            device_id=peer(s),
            device_id_type=pl.DeviceIdType.MESH,
        )

    for s in shifts:
        pass_on(s).start()
    slots = lax.broadcasted_iota(jnp.int32, (128, 128), 0)
    lanes = lax.broadcasted_iota(jnp.int32, (128, 128), 1)
    same = slots % CB == lanes % CB
    target = (here[0] * (128 // CB) + slots // CB).astype(f32)
    total = jnp.zeros((8, 128), f32)
    for s in range(ring):
        if s > 0:
            pass_on(s).wait_recv()
        block = far_ref[s]
        for h in range(2):
            hot = jnp.where((block[6 + h : 7 + h] == target) & same, 1.0, 0.0)
            mine = jnp.where(row % 2 == h, block, 0.0)
            total = total + lax.dot_general(
                mine, hot, (((1,), (1,)), ((), ())), precision=lax.Precision.HIGHEST,
                preferred_element_type=f32,
            )
    for c in range(3):
        out_ref[c : c + 1, :] = total[2 * c : 2 * c + 1] + total[2 * c + 1 : 2 * c + 2]
    for s in shifts:
        pass_on(s).wait_send()
    for n, d in enumerate(steps):
        @pl.when(inside(sizes, here, d))
        def _(n=n, d=d):
            give(n, d).wait_send()


def spread(pos, kind, sizes):
    count = len(near_steps(sizes))
    total = int(np.prod(slot_sizes(sizes)))
    return pl.pallas_call(
        functools.partial(spread_kernel, sizes),
        out_shape=jax.ShapeDtypeStruct((total, 8, 128), f32),
        in_specs=[pl.BlockSpec(memory_space=pltpu.VMEM)] * 2,
        out_specs=pl.BlockSpec(memory_space=pltpu.VMEM),
        scratch_shapes=[
            pltpu.VMEM((8, 128), f32),
            pltpu.SemaphoreType.DMA((count,)),
            pltpu.SemaphoreType.DMA((count,)),
        ],
        compiler_params=pltpu.CompilerParams(collective_id=0, has_side_effects=True),
    )(pos, kind)


def collect(part, center, mig, sizes):
    count = len(near_steps(sizes))
    dma = pltpu.SemaphoreType.DMA
    return pl.pallas_call(
        functools.partial(collect_kernel, sizes),
        out_shape=jax.ShapeDtypeStruct((3, 128), f32),
        in_specs=[pl.BlockSpec(memory_space=pltpu.VMEM)] * 3,
        out_specs=pl.BlockSpec(memory_space=pltpu.VMEM),
        scratch_shapes=[
            pltpu.VMEM((count, 8, 128), f32),
            pltpu.VMEM((sizes[0], 8, 128), f32),
            dma((count,)), dma((count,)), dma((sizes[0],)), dma((sizes[0],)),
        ],
        compiler_params=pltpu.CompilerParams(collective_id=1, has_side_effects=True),
    )(part, center, mig)


def places(sizes, nbr):
    here = tuple(lax.axis_index(n) for n in ("gx", "gy", "gz"))
    safe = jnp.where(nbr >= 0, nbr, 0)
    region = safe // 256
    step = (region // 9 - 1, region // 3 % 3 - 1, region % 3 - 1)
    slot = 0
    for n, at, d in zip(sizes, here, step):
        place = d + 1 if n >= 3 else (at + d if n == 2 else 0)
        slot = slot * min(n, 3) + place
    return slot, safe // 128 % 2, safe % 128


def sin_cos(angle):
    phi = angle - np.float32(np.pi / 2)
    sq = phi * phi
    cos_phi = 1.0
    coeffs = [1.0]
    for n in range(1, 8):
        coeffs.append(-coeffs[-1] / ((2 * n - 1) * (2 * n)))
    cos_phi = jnp.full_like(sq, coeffs[-1])
    for c in coeffs[-2::-1]:
        cos_phi = cos_phi * sq + c
    coeffs = [1.0]
    for n in range(1, 8):
        coeffs.append(-coeffs[-1] / ((2 * n) * (2 * n + 1)))
    sin_phi = jnp.full_like(sq, coeffs[-1])
    for c in coeffs[-2::-1]:
        sin_phi = sin_phi * sq + c
    sin_phi = sin_phi * phi
    return cos_phi, -sin_phi


def sigmoid(x):
    return 0.5 * jnp.tanh(0.5 * x) + 0.5


def dot(a, b):
    return jnp.dot(a, b, preferred_element_type=f32)


def geometry(sizes, nbr_ref, tab_ref, vec_s, feat_s, code_s):
    hs, eb = nbr_ref.shape
    here = tuple(lax.axis_index(n) for n in ("gx", "gy", "gz"))
    own = tab_ref[slot_of(sizes, here, (0, 0, 0))]
    block = lax.broadcasted_iota(jnp.int32, (hs, 128), 0)
    lane = lax.broadcasted_iota(jnp.int32, (hs, 128), 1)
    per_half = hs // 2
    centers = []
    for c in range(4):
        src = jnp.where(block < per_half, own[2 * c : 2 * c + 1], own[2 * c + 1 : 2 * c + 2])
        centers.append(
            jnp.concatenate(
                [
                    jnp.take_along_axis(
                        src,
                        block % per_half * CB + (h * 128 + lane) // K,
                        axis=1,
                        mode="promise_in_bounds",
                    )
                    for h in range(eb // 128)
                ],
                axis=1,
            )
        )
    nbr = nbr_ref[...]
    valid = nbr >= 0
    slot, half, lane_of = places(sizes, nbr)
    row_of = slot * 2 + half
    code_s[0] = slot
    code_s[1] = half
    code_s[2] = lane_of
    halves = eb // 128

    def look(q, acc):
        out = list(acc)
        for k in range(2):
            for c in range(4):
                src = jnp.broadcast_to(tab_ref[q, pl.ds(2 * c + k, 1), :], (hs, 128))
                for h in range(halves):
                    cols = slice(h * 128, (h + 1) * 128)
                    got = jnp.take_along_axis(
                        src, lane_of[:, cols], axis=1, mode="promise_in_bounds"
                    )
                    out[c * halves + h] = jnp.where(
                        row_of[:, cols] == 2 * q + k, got, out[c * halves + h]
                    )
        return tuple(out)

    found = lax.fori_loop(
        0,
        tab_ref.shape[0],
        look,
        tuple(jnp.zeros((hs, 128), f32) for _ in range(4 * halves)),
        unroll=2 if tab_ref.shape[0] % 2 == 0 else 1,
    )
    others = [jnp.concatenate(found[c * halves : (c + 1) * halves], axis=1) for c in range(4)]
    safe_vec = (2.0 * cutoff_radius, 0.0, 0.0)
    for c in range(3):
        vec_s[c] = jnp.where(valid, others[c] - centers[c], safe_vec[c])
    kinds_nbr = jnp.where(valid, others[3], 0.0)
    x, y, z = vec_s[0], vec_s[1], vec_s[2]
    square = x * x + y * y + z * z
    length = jnp.sqrt(square)
    inv = 1.0 / length
    ux, uy, uz = x * inv, y * inv, z * inv
    near = jnp.maximum(1.0 - square / (cutoff_radius * cutoff_radius), 0.0)
    cut = near * near
    angle = jnp.minimum(length, cutoff_radius) * np.float32(np.pi / cutoff_radius)
    sin_one, cos_one = sin_cos(angle)
    feats = [
        jnp.ones_like(x),
        sqrt_three * ux,
        sqrt_three * uy,
        sqrt_three * uz,
        sqrt_fifteen * ux * uy,
        sqrt_fifteen * uy * uz,
        0.5 * sqrt_five * (3.0 * uz * uz - 1.0),
        sqrt_fifteen * ux * uz,
        0.5 * sqrt_fifteen * (ux * ux - uy * uy),
    ]
    before, now = jnp.zeros_like(x), sin_one
    scale = radial_scale * inv * cut
    for _ in range(NB):
        feats.append(now * scale)
        before, now = now, 2.0 * cos_one * now - before
    feats.append(cut)
    for f, value in enumerate(feats):
        feat_s[:, f, :] = value.astype(bf16).astype(f32)
    base = len(feats)
    for kinds in (centers[3], kinds_nbr):
        for s in range(5):
            feat_s[:, base, :] = jnp.where(kinds == float(s), 1.0, 0.0)
            base += 1
    while base < FR:
        feat_s[:, base, :] = jnp.zeros_like(x)
        base += 1


def network(tile, lat_ref, wp, sel_y, w1, wf, wh, v2, wb, wt, wl, sel_g, wo, feat_s, grad_s, out_ref):
    first = tile * TILE_BLOCKS
    eb = lat_ref.shape[1]
    te = TILE_BLOCKS * eb
    atoms = te // K
    feat = jnp.concatenate([feat_s[first + t] for t in range(TILE_BLOCKS)], axis=1)
    feat_t = jnp.concatenate([feat, feat], axis=0).T
    env = feat_t[:, 17:18]
    feat_low = feat_t.astype(bf16)
    lat = lat_ref[...].reshape(te, lat_ref.shape[2])
    proj = dot(lat, wp[...])
    harm = dot(feat_low, sel_y[...])
    pe = proj[:, :128]
    vw = proj[:, 128:256]
    read = proj[:, 256:257]
    ew = pe * env
    norm = 1.0 / K**0.5

    def over_atom(value):
        summed = jnp.sum(value.reshape(atoms, K, 128), axis=1, keepdims=True) * norm
        return jnp.broadcast_to(summed, (atoms, K, 128)).reshape(te, 128)

    ys = [harm[:, c * 128 : (c + 1) * 128] for c in range(6)]
    envs = [over_atom(ew * yc) for yc in ys]
    ea_a = ys[0] * envs[0] + ys[1] * envs[1] + ys[2] * envs[2]
    ea_b = ys[3] * envs[3] + ys[4] * envs[4] + ys[5] * envs[5]
    inv = jnp.concatenate([(vw * ea_a).astype(bf16), (vw * ea_b).astype(bf16)], axis=1)
    p1 = dot(jnp.concatenate([lat, inv], axis=1), w1[...]) + dot(feat_low, wf[...])
    p1 = p1.astype(bf16)
    s1 = sigmoid(p1)
    h1 = p1 * s1
    d1 = s1 + h1 * (1.0 - s1)
    p2 = dot(h1.astype(bf16), wh[...])
    p2 = p2.astype(bf16)
    s2 = sigmoid(p2)
    h2 = p2 * s2
    d2 = s2 + h2 * (1.0 - s2)
    up = dot(h2.astype(bf16), v2[...])
    up = up[:, 0:1] + up[:, 1:2]
    back = dot(d2.astype(bf16), wb[...])
    g1 = ((env * env) * (d1 * back)).astype(bf16)
    gx = dot(g1, wt[...])
    gx_a, gx_b = gx[:, :128], gx[:, 128:]
    gea_a, gea_b = gx_a * vw, gx_b * vw
    gv = gx_a * ea_a + gx_b * ea_b
    gew = jnp.zeros_like(gv)
    pieces = []
    for c in range(6):
        gea = gea_a if c < 3 else gea_b
        genv = over_atom(ys[c] * gea)
        gew = gew + ys[c] * genv
        pieces.append((ew * genv + gea * envs[c]).astype(bf16))
    pieces.append(g1)
    pieces.append((pe * gew).astype(bf16))
    gf = dot(jnp.concatenate(pieces, axis=1), sel_g[...])
    lane = lax.broadcasted_iota(jnp.int32, gf.shape, 1)
    gf = gf + jnp.where(lane == 17, read + 2.0 * env * up, 0.0)
    gf = jnp.where(lane == 18, env * (read + env * up), gf)
    gft = gf.T
    for t in range(TILE_BLOCKS):
        grad_s[first + t] = gft[:, t * eb : (t + 1) * eb]
    glat = dot(
        jnp.concatenate([g1, gv.astype(bf16), (gew * env).astype(bf16)], axis=1), wl[...]
    )
    glat = glat + env * wo[...]
    out_ref[...] = glat.astype(bf16).reshape(out_ref.shape)


def pull(nbr_ref, vec_s, grad_s, edge_s, code_s, part_ref, center_ref):
    hs, eb = nbr_ref.shape
    valid = nbr_ref[...] >= 0
    x, y, z = vec_s[0], vec_s[1], vec_s[2]
    g = [grad_s[:, f, :] for f in range(19)]
    square = x * x + y * y + z * z
    length = jnp.sqrt(square)
    inv = 1.0 / length
    ux, uy, uz = x * inv, y * inv, z * inv
    near = jnp.maximum(1.0 - square / (cutoff_radius * cutoff_radius), 0.0)
    cut = near * near
    cut_d = (-4.0 / (cutoff_radius * cutoff_radius)) * length * near
    angle = jnp.minimum(length, cutoff_radius) * np.float32(np.pi / cutoff_radius)
    sin_one, cos_one = sin_cos(angle)
    sum_sin = jnp.zeros_like(x)
    sum_cos = jnp.zeros_like(x)
    s_before, s_now = jnp.zeros_like(x), sin_one
    c_before, c_now = jnp.ones_like(x), cos_one
    for n in range(1, NB + 1):
        sum_sin = sum_sin + g[8 + n] * s_now
        sum_cos = sum_cos + (n * np.pi / cutoff_radius) * (g[8 + n] * c_now)
        s_before, s_now = s_now, 2.0 * cos_one * s_now - s_before
        c_before, c_now = c_now, 2.0 * cos_one * c_now - c_before
    along = radial_scale * inv * (cut * sum_cos + (cut_d - cut * inv) * sum_sin) + g[17] * cut_d
    gx = sqrt_three * g[1] + sqrt_fifteen * (uy * g[4] + uz * g[7] + ux * g[8])
    gy = sqrt_three * g[2] + sqrt_fifteen * (ux * g[4] + uz * g[5] - uy * g[8])
    gz = sqrt_three * g[3] + sqrt_fifteen * (uy * g[5] + ux * g[7]) + 3.0 * sqrt_five * uz * g[6]
    mixed = along - (gx * ux + gy * uy + gz * uz) * inv
    for c, (gu, u) in enumerate(((gx, ux), (gy, uy), (gz, uz))):
        value = jnp.where(valid, gu * inv + u * mixed, 0.0)
        edge_s[c] = value
    edge_s[3] = g[18]

    count = part_ref.shape[0]
    row = lax.broadcasted_iota(jnp.int32, (8, eb), 0)
    lane_iota = lax.broadcasted_iota(jnp.int32, (128, eb), 0)
    atom = lax.broadcasted_iota(jnp.int32, (128, eb), 1) // K
    per_half = hs // 2
    part_ref[...] = jnp.zeros_like(part_ref)
    center_ref[...] = jnp.zeros_like(center_ref)

    def across(values, hot):
        got = lax.dot_general(
            values.astype(bf16), hot, (((1,), (1,)), ((), ())), preferred_element_type=f32
        )
        mid = got.shape[0] // 2
        return got[:mid] + got[mid:]

    def scatter(b, carry):
        slot, half, lane = (code_s[c, pl.ds(b, 1), :] for c in range(3))
        hot = jnp.where(lane_iota == lane, 1.0, 0.0).astype(bf16)
        own_hot = jnp.where(lane_iota == b % per_half * CB + atom, 1.0, 0.0).astype(bf16)
        value = edge_s[3, pl.ds(b, 1), :]
        value = jnp.broadcast_to(value, (8, eb))
        for c in range(3):
            value = jnp.where(row // 2 == c, edge_s[c, pl.ds(b, 1), :], value)
        high = value.astype(bf16).astype(f32)
        low = value - high
        own = row % 2 == b // per_half
        center_ref[...] += across(
            jnp.concatenate([jnp.where(own, high, 0.0), jnp.where(own, low, 0.0)], axis=0),
            own_hot,
        )
        there = row % 2 == half
        high = jnp.where(there, high, 0.0)
        low = jnp.where(there, low, 0.0)
        terms = [jnp.where(slot == q, high, 0.0) for q in range(count)]
        terms += [jnp.where(slot == q, low, 0.0) for q in range(count)]
        part_ref[...] += across(jnp.concatenate(terms, axis=0), hot).reshape(part_ref.shape)
        return carry

    lax.fori_loop(0, hs, scatter, 0, unroll=4)


def prepare(wlat, wten, wrad, wcen, wnei, whid, wupd, wout, sel, wp, w1, wf, v2, wb, wt, wl, sel_g, plain_s):
    tc = wten.shape[0] // 3
    wide = wlat[...].astype(f32)
    first, rest = wide[:, : 2 * tc], wide[:, 2 * tc :]
    turned = jnp.concatenate([first[:, tc:], first[:, :tc]], axis=1)
    lane = lax.broadcasted_iota(jnp.int32, first.shape, 1)
    we = jnp.where(lane < tc, first, turned)
    wv = jnp.where(lane < tc, turned, first)
    out_row = wout[...].astype(f32)
    wp[:, 0:128] = we.astype(bf16)
    wp[:, 128:256] = wv.astype(bf16)
    wp[:, 256:384] = jnp.broadcast_to(out_row, (128, out_row.shape[1])).T.astype(bf16)
    n = wide.shape[0]
    w1[0:n] = wlat[:, 2 * tc :]
    w1[n : n + 3 * tc] = wten[...]
    w1[n + 3 * tc : n + 4 * tc] = wten[2 * tc :]
    wl[0:n] = rest.T.astype(bf16)
    wl[n : n + 128] = wv.T.astype(bf16)
    wl[n + 128 : n + 256] = we.T.astype(bf16)
    ten = wten[...].astype(f32)
    wt[...] = jnp.concatenate([ten, ten[2 * tc :]], axis=0).T.astype(bf16)
    plain_s[...] = jnp.zeros_like(plain_s)
    plain_s[9:17] = wrad[...]
    sel_g[0 : sel.shape[0]] = sel[...].astype(bf16)
    at = sel.shape[0]
    sel_g[at : at + n] = plain_s[...].T.astype(bf16)
    tail = lax.broadcasted_iota(jnp.int32, (128, FR), 1)
    sel_g[at + n : at + n + 128] = jnp.where(tail == 17, 1.0, 0.0).astype(bf16)
    plain_s[18:23] = wcen[...]
    plain_s[23:28] = wnei[...]
    plain = plain_s[...]
    high = plain.astype(bf16).astype(f32)
    wf[0:FR] = high.astype(bf16)
    wf[FR : 2 * FR] = (plain - high).astype(bf16)
    col = jnp.sum(wupd[...].astype(f32) * out_row, axis=1, keepdims=True)
    col_high = col.astype(bf16).astype(f32)
    lane = lax.broadcasted_iota(jnp.int32, (n, 128), 1)
    v2[...] = jnp.where(
        lane == 0, col_high, jnp.where(lane == 1, col - col_high, 0.0)
    ).astype(bf16)
    wb[...] = (col * whid[...].astype(f32).T).astype(bf16)


def kernel(
    sizes, nbr, tab, lat, sel_y, sel, wlat, wten, wrad, wcen, wnei, whid, wupd, wout,
    out, part, center,
    vec_s, feat_s, grad_s, edge_s, code_s, wp, w1, wf, v2, wb, wt, wl, sel_g, wo, plain_s,
):
    step = pl.program_id(0)

    @pl.when(step == 0)
    def _():
        prepare(
            wlat, wten, wrad, wcen, wnei, whid, wupd, wout, sel,
            wp, w1, wf, v2, wb, wt, wl, sel_g, plain_s,
        )
        wo[...] = wout[...].astype(f32)
        geometry(sizes, nbr, tab, vec_s, feat_s, code_s)

    network(step, lat, wp, sel_y, w1, wf, whid, v2, wb, wt, wl, sel_g, wo, feat_s, grad_s, out)

    @pl.when(step == pl.num_programs(0) - 1)
    def _():
        pull(nbr, vec_s, grad_s, edge_s, code_s, part, center)


def run_device(nbr, tab, latents, weights, sizes):
    hs, eb, lat = latents.shape
    whole = lambda a: pl.BlockSpec(a.shape, lambda i, n=len(a.shape): (0,) * n)
    ops = (nbr, tab)
    wide = 128 * len(COLUMNS)
    sel_y = np.zeros((2 * FR, wide), np.float32)
    for c, pair in enumerate(COLUMNS):
        for half, m in enumerate(pair):
            if m >= 0:
                sel_y[m, c * 128 + half * 64 : c * 128 + half * 64 + 64] = 1.0
    fixed = np.zeros((wide, FR), np.float32)
    fixed[:, :9] = sel_y[:9].T
    weights = (jnp.asarray(sel_y, bf16), jnp.asarray(fixed, bf16)) + weights
    block = pl.BlockSpec((TILE_BLOCKS, eb, lat), lambda i: (i, 0, 0))
    outs = (
        jax.ShapeDtypeStruct((hs, eb, lat), bf16),
        jax.ShapeDtypeStruct(tab.shape, f32),
        jax.ShapeDtypeStruct((8, 128), f32),
    )
    return pl.pallas_call(
        functools.partial(kernel, sizes),
        out_shape=outs,
        grid=(hs // TILE_BLOCKS,),
        in_specs=[whole(a) for a in ops] + [block] + [whole(a) for a in weights],
        out_specs=[block] + [whole(a) for a in outs[1:]],
        scratch_shapes=[
            pltpu.VMEM((3, hs, eb), f32),
            pltpu.VMEM((hs, FR, eb), f32),
            pltpu.VMEM((hs, FR, eb), f32),
            pltpu.VMEM((4, hs, eb), f32),
            pltpu.VMEM((3, hs, eb), jnp.int32),
            pltpu.VMEM((lat, 384), bf16),
            pltpu.VMEM((2 * lat, lat), bf16),
            pltpu.VMEM((2 * FR, lat), bf16),
            pltpu.VMEM((lat, 128), bf16),
            pltpu.VMEM((lat, lat), bf16),
            pltpu.VMEM((lat, lat), bf16),
            pltpu.VMEM((2 * lat, lat), bf16),
            pltpu.VMEM((wide + lat + 128, FR), bf16),
            pltpu.VMEM((1, lat), f32),
            pltpu.VMEM((FR, lat), f32),
        ],
        compiler_params=pltpu.CompilerParams(vmem_limit_bytes=62 * 1024 * 1024),
        cost_estimate=pl.CostEstimate(
            flops=hs * eb * 1200000, bytes_accessed=4 * hs * eb * lat, transcendentals=0
        ),
    )(*ops, latents, *weights)


def per_device(
    positions, species, neighbors, migration, latents,
    w_latent, w_tensor, w_radial, species_center, species_neighbor, w_hidden, w_update, w_out,
):
    atom_count = positions.shape[-1]
    sizes = tuple(lax.axis_size(n) for n in ("gx", "gy", "gz"))
    weights = (
        w_latent, w_tensor, w_radial, species_center, species_neighbor, w_hidden, w_update,
        w_out[None, :],
    )
    table = spread(positions[0, 0, 0], species[0, 0], sizes)
    latent_grad, part, center = run_device(
        neighbors[0, 0, 0],
        table,
        latents[0, 0, 0],
        weights,
        sizes,
    )
    forces = collect(part, center, migration[0, 0], sizes)
    return (
        forces[None, None, None],
        center[6:8].reshape(1, 1, 1, atom_count).astype(bf16),
        latent_grad[None, None, None],
    )


def solution(mesh):
    return jax.shard_map(
        per_device,
        mesh=mesh,
        in_specs=(
            P(("parts", "gx"), "gy", "gz", None, None),
            P(("parts", "gx"), "gy", "gz", None),
            P(("parts", "gx"), "gy", "gz", None, None),
            P(("parts", "gx"), "gy", "gz", None),
            P(("parts", "gx"), "gy", "gz", None, None, None),
            P(),
            P(),
            P(),
            P(),
            P(),
            P(),
            P(),
            P(),
        ),
        out_specs=(
            P(("parts", "gx"), "gy", "gz", None, None),
            P(("parts", "gx"), "gy", "gz", None),
            P(("parts", "gx"), "gy", "gz", None, None, None),
        ),
        check_vma=False,
    )
```

```python
import functools

import jax
import jax.numpy as jnp
import numpy as np
from jax import lax
from jax.experimental import pallas as pl
from jax.experimental.pallas import tpu as pltpu
from jax.sharding import PartitionSpec as P

NB = 8
CB = 8
K = 32
FR = 32
TILE_BLOCKS = 4

cutoff_radius = 6.0
sqrt_three = 3.0**0.5
sqrt_five = 5.0**0.5
sqrt_fifteen = 15.0**0.5
radial_scale = (2.0 / cutoff_radius) ** 0.5
f32 = jnp.float32
bf16 = jnp.bfloat16

COLUMNS = ((0, 1), (-1, 2), (-1, 3), (4, 5), (6, 7), (8, -1))


def near_steps(sizes):
    spans = [(-1, 0, 1) if n > 1 else (0,) for n in sizes]
    steps = [(x, y, z) for x in spans[0] for y in spans[1] for z in spans[2]]
    return [d for d in steps if d != (0, 0, 0)]


def slot_sizes(sizes):
    return tuple(min(n, 3) for n in sizes)


def slot_of(sizes, here, step):
    index = 0
    for n, at, d in zip(sizes, here, step):
        place = d + 1 if n >= 3 else (at + d if n == 2 else 0)
        index = index * min(n, 3) + place
    return index


def inside(sizes, here, step):
    ok = None
    for n, at, d in zip(sizes, here, step):
        part = None
        if d == -1:
            part = at > 0
        elif d == 1:
            part = at < n - 1
        if part is not None:
            ok = part if ok is None else jnp.logical_and(ok, part)
    return ok


def moved(here, step):
    return {"gx": here[0] + step[0], "gy": here[1] + step[1], "gz": here[2] + step[2]}


def beside(sizes, here):
    spans = []
    for n, at in zip(sizes, here):
        low = jnp.where(at > 0, 1, 0) if n > 1 else 0
        high = jnp.where(at < n - 1, 1, 0) if n > 1 else 0
        spans.append(low + high + 1)
    return spans


def spread_kernel(sizes, pos_ref, kind_ref, out_ref, own_ref, send_sem, recv_sem):
    here = tuple(lax.axis_index(n) for n in ("gx", "gy", "gz"))
    steps = near_steps(sizes)
    out_ref[...] = jnp.zeros_like(out_ref)
    for c in range(4):
        line = pos_ref[c : c + 1, :] if c < 3 else kind_ref[...].astype(f32)
        for h in range(2):
            own_ref[2 * c + h : 2 * c + h + 1, :] = line[:, h * 128 : (h + 1) * 128]
    out_ref[slot_of(sizes, here, (0, 0, 0))] = own_ref[...]
    barrier = pltpu.get_barrier_semaphore()
    for d in steps:
        @pl.when(inside(sizes, here, d))
        def _(d=d):
            pl.semaphore_signal(
                barrier, inc=1, device_id=moved(here, d), device_id_type=pl.DeviceIdType.MESH
            )
    spans = beside(sizes, here)
    pl.semaphore_wait(barrier, spans[0] * spans[1] * spans[2] - 1)

    def copy(n, d):
        back = tuple(-v for v in d)
        there = tuple(h + v for h, v in zip(here, d))
        return pltpu.make_async_remote_copy(
            src_ref=own_ref,
            dst_ref=out_ref.at[slot_of(sizes, there, back)],
            send_sem=send_sem.at[n],
            recv_sem=recv_sem.at[n],
            device_id=moved(here, d),
            device_id_type=pl.DeviceIdType.MESH,
        )

    for n, d in enumerate(steps):
        @pl.when(inside(sizes, here, d))
        def _(n=n, d=d):
            copy(n, d).start()
    for n, d in enumerate(steps):
        @pl.when(inside(sizes, here, d))
        def _(n=n, d=d):
            copy(n, d).wait_send()
        back = tuple(-v for v in d)

        @pl.when(inside(sizes, here, back))
        def _(n=n, back=back):
            pltpu.make_async_remote_copy(
                src_ref=own_ref,
                dst_ref=out_ref.at[slot_of(sizes, here, back)],
                send_sem=send_sem.at[n],
                recv_sem=recv_sem.at[n],
                device_id=moved(here, back),
                device_id_type=pl.DeviceIdType.MESH,
            ).wait_recv()


def collect_kernel(
    sizes, part_ref, center_ref, mig_ref, out_ref, near_ref, far_ref, s1, r1, s2, r2
):
    here = tuple(lax.axis_index(n) for n in ("gx", "gy", "gz"))
    steps = near_steps(sizes)
    ring = sizes[0]
    near_ref[...] = jnp.zeros_like(near_ref)
    shifts = list(range(1, ring))

    def peer(s):
        return {"gx": lax.rem(here[0] + s, ring), "gy": here[1], "gz": here[2]}

    barrier = pltpu.get_barrier_semaphore()
    for d in steps:
        @pl.when(inside(sizes, here, d))
        def _(d=d):
            pl.semaphore_signal(
                barrier, inc=1, device_id=moved(here, d), device_id_type=pl.DeviceIdType.MESH
            )
    for gap in [g for g in range(1 - ring, ring) if abs(g) > 1]:
        @pl.when(jnp.logical_and(here[0] + gap >= 0, here[0] + gap < ring))
        def _(gap=gap):
            pl.semaphore_signal(
                barrier,
                inc=1,
                device_id=moved(here, (gap, 0, 0)),
                device_id_type=pl.DeviceIdType.MESH,
            )
    spans = beside(sizes, here)
    pl.semaphore_wait(barrier, spans[0] * spans[1] * spans[2] - 1 + ring - spans[0])

    def give(n, d):
        return pltpu.make_async_remote_copy(
            src_ref=part_ref.at[slot_of(sizes, here, d)],
            dst_ref=near_ref.at[n],
            send_sem=s1.at[n],
            recv_sem=r1.at[n],
            device_id=moved(here, d),
            device_id_type=pl.DeviceIdType.MESH,
        )

    for n, d in enumerate(steps):
        @pl.when(inside(sizes, here, d))
        def _(n=n, d=d):
            give(n, d).start()
    for n, d in enumerate(steps):
        back = tuple(-v for v in d)

        @pl.when(inside(sizes, here, back))
        def _(n=n, back=back):
            pltpu.make_async_remote_copy(
                src_ref=center_ref,
                dst_ref=near_ref.at[n],
                send_sem=s1.at[n],
                recv_sem=r1.at[n],
                device_id=moved(here, back),
                device_id_type=pl.DeviceIdType.MESH,
            ).wait_recv()
    force = center_ref[...] - part_ref[slot_of(sizes, here, (0, 0, 0))]
    for n in range(len(steps)):
        force = force - near_ref[n]
    row = lax.broadcasted_iota(jnp.int32, force.shape, 0)
    hs = mig_ref.shape[1]
    kept = lax.broadcasted_iota(jnp.int32, (8, hs), 1) // (hs // 2) == (
        lax.broadcasted_iota(jnp.int32, (8, hs), 0) % 2
    )
    mig = jnp.where(kept, mig_ref[...].astype(f32), 0.0)
    widen = (
        lax.broadcasted_iota(jnp.int32, (hs, 128), 1) // CB
        == lax.broadcasted_iota(jnp.int32, (hs, 128), 0) % (hs // 2)
    )
    mig = jnp.dot(
        mig, jnp.where(widen, 1.0, 0.0), precision=lax.Precision.HIGHEST,
        preferred_element_type=f32,
    )
    force = jnp.where(row >= 6, mig, force)
    far_ref[0] = force

    def pass_on(s):
        return pltpu.make_async_remote_copy(
            src_ref=far_ref.at[0],
            dst_ref=far_ref.at[s],
            send_sem=s2.at[s],
            recv_sem=r2.at[s],
            device_id=peer(s),
            device_id_type=pl.DeviceIdType.MESH,
        )

    for s in shifts:
        pass_on(s).start()
    slots = lax.broadcasted_iota(jnp.int32, (128, 128), 0)
    lanes = lax.broadcasted_iota(jnp.int32, (128, 128), 1)
    same = slots % CB == lanes % CB
    target = (here[0] * (128 // CB) + slots // CB).astype(f32)
    total = jnp.zeros((8, 128), f32)
    for s in range(ring):
        if s > 0:
            pass_on(s).wait_recv()
        block = far_ref[s]
        for h in range(2):
            hot = jnp.where((block[6 + h : 7 + h] == target) & same, 1.0, 0.0)
            mine = jnp.where(row % 2 == h, block, 0.0)
            total = total + lax.dot_general(
                mine, hot, (((1,), (1,)), ((), ())), precision=lax.Precision.HIGHEST,
                preferred_element_type=f32,
            )
    for c in range(3):
        out_ref[c : c + 1, :] = total[2 * c : 2 * c + 1] + total[2 * c + 1 : 2 * c + 2]
    for s in shifts:
        pass_on(s).wait_send()
    for n, d in enumerate(steps):
        @pl.when(inside(sizes, here, d))
        def _(n=n, d=d):
            give(n, d).wait_send()


def spread(pos, kind, sizes):
    count = len(near_steps(sizes))
    total = int(np.prod(slot_sizes(sizes)))
    return pl.pallas_call(
        functools.partial(spread_kernel, sizes),
        out_shape=jax.ShapeDtypeStruct((total, 8, 128), f32),
        in_specs=[pl.BlockSpec(memory_space=pltpu.VMEM)] * 2,
        out_specs=pl.BlockSpec(memory_space=pltpu.VMEM),
        scratch_shapes=[
            pltpu.VMEM((8, 128), f32),
            pltpu.SemaphoreType.DMA((count,)),
            pltpu.SemaphoreType.DMA((count,)),
        ],
        compiler_params=pltpu.CompilerParams(collective_id=0, has_side_effects=True),
    )(pos, kind)


def collect(part, center, mig, sizes):
    count = len(near_steps(sizes))
    dma = pltpu.SemaphoreType.DMA
    return pl.pallas_call(
        functools.partial(collect_kernel, sizes),
        out_shape=jax.ShapeDtypeStruct((3, 128), f32),
        in_specs=[pl.BlockSpec(memory_space=pltpu.VMEM)] * 3,
        out_specs=pl.BlockSpec(memory_space=pltpu.VMEM),
        scratch_shapes=[
            pltpu.VMEM((count, 8, 128), f32),
            pltpu.VMEM((sizes[0], 8, 128), f32),
            dma((count,)), dma((count,)), dma((sizes[0],)), dma((sizes[0],)),
        ],
        compiler_params=pltpu.CompilerParams(collective_id=1, has_side_effects=True),
    )(part, center, mig)


def places(sizes, nbr):
    here = tuple(lax.axis_index(n) for n in ("gx", "gy", "gz"))
    safe = jnp.where(nbr >= 0, nbr, 0)
    region = safe // 256
    step = (region // 9 - 1, region // 3 % 3 - 1, region % 3 - 1)
    slot = 0
    for n, at, d in zip(sizes, here, step):
        place = d + 1 if n >= 3 else (at + d if n == 2 else 0)
        slot = slot * min(n, 3) + place
    return slot, safe // 128 % 2, safe % 128


def sin_cos(angle):
    phi = angle - np.float32(np.pi / 2)
    sq = phi * phi
    cos_phi = 1.0
    coeffs = [1.0]
    for n in range(1, 8):
        coeffs.append(-coeffs[-1] / ((2 * n - 1) * (2 * n)))
    cos_phi = jnp.full_like(sq, coeffs[-1])
    for c in coeffs[-2::-1]:
        cos_phi = cos_phi * sq + c
    coeffs = [1.0]
    for n in range(1, 8):
        coeffs.append(-coeffs[-1] / ((2 * n) * (2 * n + 1)))
    sin_phi = jnp.full_like(sq, coeffs[-1])
    for c in coeffs[-2::-1]:
        sin_phi = sin_phi * sq + c
    sin_phi = sin_phi * phi
    return cos_phi, -sin_phi


def sigmoid(x):
    return 0.5 * jnp.tanh(0.5 * x) + 0.5


def dot(a, b):
    return jnp.dot(a, b, preferred_element_type=f32)


def geometry(sizes, nbr_ref, tab_ref, vec_s, feat_s, code_s):
    hs, eb = nbr_ref.shape
    here = tuple(lax.axis_index(n) for n in ("gx", "gy", "gz"))
    own = tab_ref[slot_of(sizes, here, (0, 0, 0))]
    block = lax.broadcasted_iota(jnp.int32, (hs, 128), 0)
    lane = lax.broadcasted_iota(jnp.int32, (hs, 128), 1)
    per_half = hs // 2
    centers = []
    for c in range(4):
        src = jnp.where(block < per_half, own[2 * c : 2 * c + 1], own[2 * c + 1 : 2 * c + 2])
        centers.append(
            jnp.concatenate(
                [
                    jnp.take_along_axis(
                        src,
                        block % per_half * CB + (h * 128 + lane) // K,
                        axis=1,
                        mode="promise_in_bounds",
                    )
                    for h in range(eb // 128)
                ],
                axis=1,
            )
        )
    nbr = nbr_ref[...]
    valid = nbr >= 0
    slot, half, lane_of = places(sizes, nbr)
    row_of = slot * 2 + half
    code_s[0] = slot
    code_s[1] = half
    code_s[2] = lane_of
    halves = eb // 128

    def look(q, acc):
        out = list(acc)
        for k in range(2):
            for c in range(4):
                src = jnp.broadcast_to(tab_ref[q, pl.ds(2 * c + k, 1), :], (hs, 128))
                for h in range(halves):
                    cols = slice(h * 128, (h + 1) * 128)
                    got = jnp.take_along_axis(
                        src, lane_of[:, cols], axis=1, mode="promise_in_bounds"
                    )
                    out[c * halves + h] = jnp.where(
                        row_of[:, cols] == 2 * q + k, got, out[c * halves + h]
                    )
        return tuple(out)

    found = lax.fori_loop(
        0,
        tab_ref.shape[0],
        look,
        tuple(jnp.zeros((hs, 128), f32) for _ in range(4 * halves)),
        unroll=2 if tab_ref.shape[0] % 2 == 0 else 1,
    )
    others = [jnp.concatenate(found[c * halves : (c + 1) * halves], axis=1) for c in range(4)]
    safe_vec = (2.0 * cutoff_radius, 0.0, 0.0)
    for c in range(3):
        vec_s[c] = jnp.where(valid, others[c] - centers[c], safe_vec[c])
    kinds_nbr = jnp.where(valid, others[3], 0.0)
    x, y, z = vec_s[0], vec_s[1], vec_s[2]
    square = x * x + y * y + z * z
    length = jnp.sqrt(square)
    inv = 1.0 / length
    ux, uy, uz = x * inv, y * inv, z * inv
    near = jnp.maximum(1.0 - square / (cutoff_radius * cutoff_radius), 0.0)
    cut = near * near
    angle = jnp.minimum(length, cutoff_radius) * np.float32(np.pi / cutoff_radius)
    sin_one, cos_one = sin_cos(angle)
    feats = [
        jnp.ones_like(x),
        sqrt_three * ux,
        sqrt_three * uy,
        sqrt_three * uz,
        sqrt_fifteen * ux * uy,
        sqrt_fifteen * uy * uz,
        0.5 * sqrt_five * (3.0 * uz * uz - 1.0),
        sqrt_fifteen * ux * uz,
        0.5 * sqrt_fifteen * (ux * ux - uy * uy),
    ]
    before, now = jnp.zeros_like(x), sin_one
    scale = radial_scale * inv * cut
    for _ in range(NB):
        feats.append(now * scale)
        before, now = now, 2.0 * cos_one * now - before
    feats.append(cut)
    for f, value in enumerate(feats):
        feat_s[:, f, :] = value.astype(bf16).astype(f32)
    base = len(feats)
    for kinds in (centers[3], kinds_nbr):
        for s in range(5):
            feat_s[:, base, :] = jnp.where(kinds == float(s), 1.0, 0.0)
            base += 1
    while base < FR:
        feat_s[:, base, :] = jnp.zeros_like(x)
        base += 1


def network(tile, lat_ref, wp, sel_y, w1, wf, wh, v2, wb, wt, wl, sel_g, wo, feat_s, grad_s, out_ref):
    first = tile * TILE_BLOCKS
    eb = lat_ref.shape[1]
    te = TILE_BLOCKS * eb
    atoms = te // K
    feat = jnp.concatenate([feat_s[first + t] for t in range(TILE_BLOCKS)], axis=1)
    feat_t = jnp.concatenate([feat, feat], axis=0).T
    env = feat_t[:, 17:18]
    feat_low = feat_t.astype(bf16)
    lat = lat_ref[...].reshape(te, lat_ref.shape[2])
    proj = dot(lat, wp[...])
    harm = dot(feat_low, sel_y[...])
    pe = proj[:, :128]
    vw = proj[:, 128:256]
    read = proj[:, 256:257]
    ew = pe * env
    norm = 1.0 / K**0.5

    def over_atom(value):
        summed = jnp.sum(value.reshape(atoms, K, 128), axis=1, keepdims=True) * norm
        return jnp.broadcast_to(summed, (atoms, K, 128)).reshape(te, 128)

    ys = [harm[:, c * 128 : (c + 1) * 128] for c in range(6)]
    envs = [over_atom(ew * yc) for yc in ys]
    ea_a = ys[0] * envs[0] + ys[1] * envs[1] + ys[2] * envs[2]
    ea_b = ys[3] * envs[3] + ys[4] * envs[4] + ys[5] * envs[5]
    inv = jnp.concatenate([(vw * ea_a).astype(bf16), (vw * ea_b).astype(bf16)], axis=1)
    p1 = dot(jnp.concatenate([lat, inv], axis=1), w1[...]) + dot(feat_low, wf[...])
    p1 = p1.astype(bf16)
    s1 = sigmoid(p1)
    h1 = p1 * s1
    d1 = s1 + h1 * (1.0 - s1)
    p2 = dot(h1.astype(bf16), wh[...])
    p2 = p2.astype(bf16)
    s2 = sigmoid(p2)
    h2 = p2 * s2
    d2 = s2 + h2 * (1.0 - s2)
    up = dot(h2.astype(bf16), v2[...])
    up = up[:, 0:1] + up[:, 1:2]
    back = dot(d2.astype(bf16), wb[...])
    g1 = ((env * env) * (d1 * back)).astype(bf16)
    gx = dot(g1, wt[...])
    gx_a, gx_b = gx[:, :128], gx[:, 128:]
    gea_a, gea_b = gx_a * vw, gx_b * vw
    gv = gx_a * ea_a + gx_b * ea_b
    gew = jnp.zeros_like(gv)
    pieces = []
    for c in range(6):
        gea = gea_a if c < 3 else gea_b
        genv = over_atom(ys[c] * gea)
        gew = gew + ys[c] * genv
        pieces.append((ew * genv + gea * envs[c]).astype(bf16))
    pieces.append(g1)
    pieces.append((pe * gew).astype(bf16))
    gf = dot(jnp.concatenate(pieces, axis=1), sel_g[...])
    lane = lax.broadcasted_iota(jnp.int32, gf.shape, 1)
    gf = gf + jnp.where(lane == 17, read + 2.0 * env * up, 0.0)
    gf = jnp.where(lane == 18, env * (read + env * up), gf)
    gft = gf.T
    for t in range(TILE_BLOCKS):
        grad_s[first + t] = gft[:, t * eb : (t + 1) * eb]
    glat = dot(
        jnp.concatenate([g1, gv.astype(bf16), (gew * env).astype(bf16)], axis=1), wl[...]
    )
    glat = glat + env * wo[...]
    out_ref[...] = glat.astype(bf16).reshape(out_ref.shape)


def pull(nbr_ref, vec_s, grad_s, edge_s, code_s, part_ref, center_ref):
    hs, eb = nbr_ref.shape
    valid = nbr_ref[...] >= 0
    x, y, z = vec_s[0], vec_s[1], vec_s[2]
    g = [grad_s[:, f, :] for f in range(19)]
    square = x * x + y * y + z * z
    length = jnp.sqrt(square)
    inv = 1.0 / length
    ux, uy, uz = x * inv, y * inv, z * inv
    near = jnp.maximum(1.0 - square / (cutoff_radius * cutoff_radius), 0.0)
    cut = near * near
    cut_d = (-4.0 / (cutoff_radius * cutoff_radius)) * length * near
    angle = jnp.minimum(length, cutoff_radius) * np.float32(np.pi / cutoff_radius)
    sin_one, cos_one = sin_cos(angle)
    sum_sin = jnp.zeros_like(x)
    sum_cos = jnp.zeros_like(x)
    s_before, s_now = jnp.zeros_like(x), sin_one
    c_before, c_now = jnp.ones_like(x), cos_one
    for n in range(1, NB + 1):
        sum_sin = sum_sin + g[8 + n] * s_now
        sum_cos = sum_cos + (n * np.pi / cutoff_radius) * (g[8 + n] * c_now)
        s_before, s_now = s_now, 2.0 * cos_one * s_now - s_before
        c_before, c_now = c_now, 2.0 * cos_one * c_now - c_before
    along = radial_scale * inv * (cut * sum_cos + (cut_d - cut * inv) * sum_sin) + g[17] * cut_d
    gx = sqrt_three * g[1] + sqrt_fifteen * (uy * g[4] + uz * g[7] + ux * g[8])
    gy = sqrt_three * g[2] + sqrt_fifteen * (ux * g[4] + uz * g[5] - uy * g[8])
    gz = sqrt_three * g[3] + sqrt_fifteen * (uy * g[5] + ux * g[7]) + 3.0 * sqrt_five * uz * g[6]
    mixed = along - (gx * ux + gy * uy + gz * uz) * inv
    for c, (gu, u) in enumerate(((gx, ux), (gy, uy), (gz, uz))):
        value = jnp.where(valid, gu * inv + u * mixed, 0.0)
        edge_s[c] = value
    edge_s[3] = g[18]

    count = part_ref.shape[0]
    row = lax.broadcasted_iota(jnp.int32, (8, eb), 0)
    lane_iota = lax.broadcasted_iota(jnp.int32, (128, eb), 0)
    atom = lax.broadcasted_iota(jnp.int32, (128, eb), 1) // K
    per_half = hs // 2
    part_ref[...] = jnp.zeros_like(part_ref)
    center_ref[...] = jnp.zeros_like(center_ref)

    def across(values, hot):
        got = lax.dot_general(
            values.astype(bf16), hot, (((1,), (1,)), ((), ())), preferred_element_type=f32
        )
        mid = got.shape[0] // 2
        return got[:mid] + got[mid:]

    def scatter(b, carry):
        slot, half, lane = (code_s[c, pl.ds(b, 1), :] for c in range(3))
        hot = jnp.where(lane_iota == lane, 1.0, 0.0).astype(bf16)
        own_hot = jnp.where(lane_iota == b % per_half * CB + atom, 1.0, 0.0).astype(bf16)
        value = edge_s[3, pl.ds(b, 1), :]
        value = jnp.broadcast_to(value, (8, eb))
        for c in range(3):
            value = jnp.where(row // 2 == c, edge_s[c, pl.ds(b, 1), :], value)
        high = value.astype(bf16).astype(f32)
        low = value - high
        own = row % 2 == b // per_half
        center_ref[...] += across(
            jnp.concatenate([jnp.where(own, high, 0.0), jnp.where(own, low, 0.0)], axis=0),
            own_hot,
        )
        there = row % 2 == half
        high = jnp.where(there, high, 0.0)
        low = jnp.where(there, low, 0.0)
        terms = [jnp.where(slot == q, high, 0.0) for q in range(count)]
        terms += [jnp.where(slot == q, low, 0.0) for q in range(count)]
        part_ref[...] += across(jnp.concatenate(terms, axis=0), hot).reshape(part_ref.shape)
        return carry

    lax.fori_loop(0, hs, scatter, 0, unroll=4)


def prepare(wlat, wten, wrad, wcen, wnei, whid, wupd, wout, sel, wp, w1, wf, v2, wb, wt, wl, sel_g, plain_s):
    tc = wten.shape[0] // 3
    wide = wlat[...].astype(f32)
    first, rest = wide[:, : 2 * tc], wide[:, 2 * tc :]
    turned = jnp.concatenate([first[:, tc:], first[:, :tc]], axis=1)
    lane = lax.broadcasted_iota(jnp.int32, first.shape, 1)
    we = jnp.where(lane < tc, first, turned)
    wv = jnp.where(lane < tc, turned, first)
    out_row = wout[...].astype(f32)
    wp[:, 0:128] = we.astype(bf16)
    wp[:, 128:256] = wv.astype(bf16)
    wp[:, 256:384] = jnp.broadcast_to(out_row, (128, out_row.shape[1])).T.astype(bf16)
    n = wide.shape[0]
    w1[0:n] = wlat[:, 2 * tc :]
    w1[n : n + 3 * tc] = wten[...]
    w1[n + 3 * tc : n + 4 * tc] = wten[2 * tc :]
    wl[0:n] = rest.T.astype(bf16)
    wl[n : n + 128] = wv.T.astype(bf16)
    wl[n + 128 : n + 256] = we.T.astype(bf16)
    ten = wten[...].astype(f32)
    wt[...] = jnp.concatenate([ten, ten[2 * tc :]], axis=0).T.astype(bf16)
    plain_s[...] = jnp.zeros_like(plain_s)
    plain_s[9:17] = wrad[...]
    sel_g[0 : sel.shape[0]] = sel[...].astype(bf16)
    at = sel.shape[0]
    sel_g[at : at + n] = plain_s[...].T.astype(bf16)
    tail = lax.broadcasted_iota(jnp.int32, (128, FR), 1)
    sel_g[at + n : at + n + 128] = jnp.where(tail == 17, 1.0, 0.0).astype(bf16)
    plain_s[18:23] = wcen[...]
    plain_s[23:28] = wnei[...]
    plain = plain_s[...]
    high = plain.astype(bf16).astype(f32)
    wf[0:FR] = high.astype(bf16)
    wf[FR : 2 * FR] = (plain - high).astype(bf16)
    col = jnp.sum(wupd[...].astype(f32) * out_row, axis=1, keepdims=True)
    col_high = col.astype(bf16).astype(f32)
    lane = lax.broadcasted_iota(jnp.int32, (n, 128), 1)
    v2[...] = jnp.where(
        lane == 0, col_high, jnp.where(lane == 1, col - col_high, 0.0)
    ).astype(bf16)
    wb[...] = (col * whid[...].astype(f32).T).astype(bf16)


def kernel(
    sizes, nbr, tab, lat, sel_y, sel, wlat, wten, wrad, wcen, wnei, whid, wupd, wout,
    out, part, center, energy,
    vec_s, feat_s, grad_s, edge_s, code_s, wp, w1, wf, v2, wb, wt, wl, sel_g, wo, plain_s,
):
    step = pl.program_id(0)

    @pl.when(step == 0)
    def _():
        prepare(
            wlat, wten, wrad, wcen, wnei, whid, wupd, wout, sel,
            wp, w1, wf, v2, wb, wt, wl, sel_g, plain_s,
        )
        wo[...] = wout[...].astype(f32)
        geometry(sizes, nbr, tab, vec_s, feat_s, code_s)

    network(step, lat, wp, sel_y, w1, wf, whid, v2, wb, wt, wl, sel_g, wo, feat_s, grad_s, out)

    @pl.when(step == pl.num_programs(0) - 1)
    def _():
        pull(nbr, vec_s, grad_s, edge_s, code_s, part, center)
        energy[...] = jnp.concatenate([center[6:7], center[7:8]], axis=1).astype(bf16)


def run_device(nbr, tab, latents, weights, sizes):
    hs, eb, lat = latents.shape
    whole = lambda a: pl.BlockSpec(a.shape, lambda i, n=len(a.shape): (0,) * n)
    ops = (nbr, tab)
    wide = 128 * len(COLUMNS)
    sel_y = np.zeros((2 * FR, wide), np.float32)
    for c, pair in enumerate(COLUMNS):
        for half, m in enumerate(pair):
            if m >= 0:
                sel_y[m, c * 128 + half * 64 : c * 128 + half * 64 + 64] = 1.0
    fixed = np.zeros((wide, FR), np.float32)
    fixed[:, :9] = sel_y[:9].T
    weights = (jnp.asarray(sel_y, bf16), jnp.asarray(fixed, bf16)) + weights
    block = pl.BlockSpec((TILE_BLOCKS, eb, lat), lambda i: (i, 0, 0))
    outs = (
        jax.ShapeDtypeStruct((hs, eb, lat), bf16),
        jax.ShapeDtypeStruct(tab.shape, f32),
        jax.ShapeDtypeStruct((8, 128), f32),
        jax.ShapeDtypeStruct((1, hs * CB), bf16),
    )
    return pl.pallas_call(
        functools.partial(kernel, sizes),
        out_shape=outs,
        grid=(hs // TILE_BLOCKS,),
        in_specs=[whole(a) for a in ops] + [block] + [whole(a) for a in weights],
        out_specs=[block] + [whole(a) for a in outs[1:]],
        scratch_shapes=[
            pltpu.VMEM((3, hs, eb), f32),
            pltpu.VMEM((hs, FR, eb), f32),
            pltpu.VMEM((hs, FR, eb), f32),
            pltpu.VMEM((4, hs, eb), f32),
            pltpu.VMEM((3, hs, eb), jnp.int32),
            pltpu.VMEM((lat, 384), bf16),
            pltpu.VMEM((2 * lat, lat), bf16),
            pltpu.VMEM((2 * FR, lat), bf16),
            pltpu.VMEM((lat, 128), bf16),
            pltpu.VMEM((lat, lat), bf16),
            pltpu.VMEM((lat, lat), bf16),
            pltpu.VMEM((2 * lat, lat), bf16),
            pltpu.VMEM((wide + lat + 128, FR), bf16),
            pltpu.VMEM((1, lat), f32),
            pltpu.VMEM((FR, lat), f32),
        ],
        compiler_params=pltpu.CompilerParams(vmem_limit_bytes=62 * 1024 * 1024),
        cost_estimate=pl.CostEstimate(
            flops=hs * eb * 1200000, bytes_accessed=4 * hs * eb * lat, transcendentals=0
        ),
    )(*ops, latents, *weights)


def per_device(
    positions, species, neighbors, migration, latents,
    w_latent, w_tensor, w_radial, species_center, species_neighbor, w_hidden, w_update, w_out,
):
    atom_count = positions.shape[-1]
    sizes = tuple(lax.axis_size(n) for n in ("gx", "gy", "gz"))
    weights = (
        w_latent, w_tensor, w_radial, species_center, species_neighbor, w_hidden, w_update,
        w_out.astype(f32).reshape(1, -1),
    )
    table = spread(positions[0, 0, 0], species[0, 0], sizes)
    latent_grad, part, center, energy = run_device(
        neighbors[0, 0, 0],
        table,
        latents[0, 0, 0],
        weights,
        sizes,
    )
    forces = collect(part, center, migration[0, 0], sizes)
    return (
        forces[None, None, None],
        energy.reshape(1, 1, 1, atom_count),
        latent_grad[None, None, None],
    )


def solution(mesh):
    return jax.shard_map(
        per_device,
        mesh=mesh,
        in_specs=(
            P(("parts", "gx"), "gy", "gz", None, None),
            P(("parts", "gx"), "gy", "gz", None),
            P(("parts", "gx"), "gy", "gz", None, None),
            P(("parts", "gx"), "gy", "gz", None),
            P(("parts", "gx"), "gy", "gz", None, None, None),
            P(),
            P(),
            P(),
            P(),
            P(),
            P(),
            P(),
            P(),
        ),
        out_specs=(
            P(("parts", "gx"), "gy", "gz", None, None),
            P(("parts", "gx"), "gy", "gz", None),
            P(("parts", "gx"), "gy", "gz", None, None, None),
        ),
        check_vma=False,
    )
```
